256 devices in a mesh: gx: 8 (over x_lo, y), gy: 8 (over z), gz: 4 (over x_hi, core).
Axes of the slice: x: 4 (x_hi: 2, x_lo: 2; x = x_hi * 2 + x_lo), y: 4, z: 8, core: 2. Of those that a mesh axis runs over, the one named last changes fastest.
Arguments:
- out_grad: bfloat16 [4096, 16384], P('gx', ('gy', 'gz')), may hold values from -0.09375 to 0.09375
- layer_input: bfloat16 [4096, 16384], P('gx', ('gy', 'gz')), may hold values from -6 to 6
- out_weight: bfloat16 [16384, 16384], P(('gy', 'gz'), 'gx'), may hold values from -0.046875 to 0.046875
- saved_queries: bfloat16 [4096, 16384], P('gx', ('gy', 'gz'))
- saved_keys: bfloat16 [4096, 1024], P('gx')
- saved_values: bfloat16 [4096, 1024], P('gx'), may hold values from -6 to 6
- query_down: bfloat16 [16384, 32], P(('gy', 'gz')), may hold values from -0.046875 to 0.046875
- query_up: bfloat16 [32, 16384], P(None, ('gy', 'gz')), may hold values from -0.046875 to 0.046875
- value_down: bfloat16 [16384, 32], P(('gy', 'gz')), may hold values from -0.046875 to 0.046875
- value_up: bfloat16 [32, 1024], replicated, may hold values from -0.1875 to 0.1875
- lengths: int32 [8], P('gx'), may hold values from 128 to 512, as said below
Outputs:
- query_down_grad: float32 [16384, 32], P(('gy', 'gz'))
- query_up_grad: float32 [32, 16384], P(None, ('gy', 'gz'))
- value_down_grad: float32 [16384, 32], P(('gy', 'gz'))
- value_up_grad: float32 [32, 1024], replicated
The draws below stay inside these ranges and needn't reach their ends.
Inputs may be any that keep to these rules, and one draw needn't show every extreme that they name: `lengths`: at least one sequence of each draw is full.
All inputs are finite; a program needn't handle non-finite values.
Results may differ from the reference program's by a relative error of at most 0.0042.
Values may be sent and summed in bfloat16 or wider, within the bound.
A program may use at most 128 MiB of HBM per device.

```python
import jax
import jax.numpy as jnp
from jax import lax

D = 16384
HQ = 128
KVH = 8
HD = 128
R = 32
SEQ = 512
SEQS = 8
TOKENS = 4096


def pair_base(key):
    base_key = jax.random.fold_in(key, 101)
    first_key, second_key = jax.random.split(base_key)
    query_rows = jax.random.normal(first_key, (TOKENS, HQ * HD), jnp.float32)
    key_rows = jax.random.normal(second_key, (TOKENS, KVH * HD), jnp.float32)
    return (query_rows, key_rows)


def draw_saved_queries(key, part):
    query_rows, key_rows = pair_base(key)
    return query_rows.astype(jnp.bfloat16)


def draw_saved_keys(key, part):
    query_rows, key_rows = pair_base(key)
    return key_rows.astype(jnp.bfloat16)


def draw_lengths(key, part):
    key = jax.random.fold_in(key, 7)
    first_key, second_key = jax.random.split(key)
    drawn_lengths = jax.random.randint(first_key, (SEQS,), SEQ // 4, SEQ + 1)
    full_index = jax.random.randint(second_key, (), 0, SEQS)
    return jnp.where(jnp.arange(SEQS) == full_index, SEQ, drawn_lengths).astype(jnp.int32)


def shard_levels(stream_key, extent, cuts, low, top_value):
    factor_of, own = 1.0, jax.random.fold_in(stream_key, 6)
    for axis_at, parts in cuts:
        steps = jnp.exp(jax.random.uniform(jax.random.fold_in(own, axis_at), (parts,), jnp.float32, low / len(cuts), top_value / len(cuts)))
        factor_of = factor_of * jnp.repeat(steps, extent[axis_at] // parts).reshape([-1 if axis == axis_at else 1 for axis in range(len(extent))])
    return factor_of


def scatter_about(key, shape, width, most, shards=(), kind=jnp.bfloat16):
    values = width * jax.random.normal(key, shape, jnp.float32)
    if shards:
        values = values * shard_levels(key, shape, shards, -0.22, 0.18)
    return jnp.clip(values, -most, most).astype(kind)


def setup_inputs(seed: int = 0) -> dict:
    key_list = jax.random.split(jax.random.key(seed), 12)
    out_grad = scatter_about(key_list[0], (TOKENS, D), TOKENS ** -0.5, 0.09375, ((0, 8), (1, 32)))
    layer_input = scatter_about(key_list[1], (TOKENS, D), 1.0, 6.0, ((0, 8), (1, 32)))
    out_weight = scatter_about(key_list[2], (HQ * HD, D), D ** -0.5, 0.046875, ((0, 32), (1, 8)))
    saved_queries = draw_saved_queries(jax.random.fold_in(key_list[11], 71), 0)
    saved_keys = draw_saved_keys(jax.random.fold_in(key_list[11], 71), 0)
    saved_values = scatter_about(key_list[5], (TOKENS, KVH * HD), 1.0, 6.0, ((0, 8),))
    query_down = scatter_about(key_list[6], (D, R), D ** -0.5, 0.046875, ((0, 32),))
    query_up = scatter_about(key_list[7], (R, HQ * HD), (HQ * HD) ** -0.5, 0.046875, ((1, 32),))
    value_down = scatter_about(key_list[8], (D, R), D ** -0.5, 0.046875, ((0, 32),))
    value_up = scatter_about(key_list[9], (R, KVH * HD), (KVH * HD) ** -0.5, 0.1875)
    lengths = draw_lengths(jax.random.fold_in(key_list[11], 71), 0)
    return dict(out_grad=out_grad, layer_input=layer_input, out_weight=out_weight, saved_queries=saved_queries, saved_keys=saved_keys, saved_values=saved_values, query_down=query_down, query_up=query_up, value_down=value_down, value_up=value_up, lengths=lengths)


adapter_scale = 2.0
mask_fill = -1.0e30
highest = lax.Precision.HIGHEST


def precise_product(left_side, right_side):
    return jnp.dot(left_side, right_side, precision=highest, preferred_element_type=jnp.float32)


def one_sequence(sequence_items):
    query_rows, key_rows, value_rows, grad_rows, length = sequence_items
    group_size = HQ // KVH
    position = jnp.arange(SEQ)
    visible = (position[None, :] <= position[:, None]) & (position[None, :] < length)
    query_heads = query_rows.astype(jnp.float32).reshape(SEQ, KVH, group_size, HD)
    head_keys = key_rows.astype(jnp.float32).reshape(SEQ, KVH, HD)
    head_values = value_rows.astype(jnp.float32).reshape(SEQ, KVH, HD)
    grad_heads = grad_rows.astype(jnp.float32).reshape(SEQ, KVH, group_size, HD)
    score_scale = HD ** -0.5
    scores = jnp.einsum("qkgd,pkd->kgqp", query_heads, head_keys, precision=highest) * score_scale
    scores = jnp.where(visible, scores, mask_fill)
    largest = jnp.max(scores, axis=-1, keepdims=True)
    raised = jnp.exp(scores - largest)
    attention = raised / jnp.sum(raised, axis=-1, keepdims=True)
    attention_low = lax.optimization_barrier(attention.astype(jnp.bfloat16)).astype(jnp.float32)
    value_gradient = jnp.einsum("kgqp,qkgd->pkd", attention_low, grad_heads, precision=highest)
    prob_grad = jnp.einsum("qkgd,pkd->kgqp", grad_heads, head_values, precision=highest)
    centre = jnp.sum(attention * prob_grad, axis=-1, keepdims=True)
    score_grad = lax.optimization_barrier((attention * (prob_grad - centre)).astype(jnp.bfloat16)).astype(jnp.float32)
    query_gradient = jnp.einsum("kgqp,pkd->qkgd", score_grad, head_keys, precision=highest) * score_scale
    return query_gradient.reshape(SEQ, HQ * HD), value_gradient.reshape(SEQ, KVH * HD)


def reference(out_grad, layer_input, out_weight, saved_queries, saved_keys, saved_values, query_down, query_up, value_down, value_up, lengths):
    attn_full = precise_product(out_grad.astype(jnp.float32), out_weight.astype(jnp.float32).T)
    position = jnp.arange(TOKENS) % SEQ
    limit_rows = jnp.repeat(lengths, SEQ)
    attn_grad = jnp.where((position < limit_rows)[:, None], attn_full, 0.0).astype(jnp.bfloat16)
    query_gradient, value_gradient = lax.map(one_sequence, (
        saved_queries.reshape(SEQS, SEQ, HQ * HD),
        saved_keys.reshape(SEQS, SEQ, KVH * HD),
        saved_values.reshape(SEQS, SEQ, KVH * HD),
        attn_grad.reshape(SEQS, SEQ, HQ * HD),
        lengths))
    query_gradient = query_gradient.reshape(TOKENS, HQ * HD)
    value_gradient = value_gradient.reshape(TOKENS, KVH * HD)
    broad_input = layer_input.astype(jnp.float32)
    query_middle = precise_product(broad_input, query_down.astype(jnp.float32))
    value_middle = precise_product(broad_input, value_down.astype(jnp.float32))
    query_adapter_factor = precise_product(query_gradient, query_up.astype(jnp.float32).T)
    value_adapter_factor = precise_product(value_gradient, value_up.astype(jnp.float32).T)
    return (adapter_scale * precise_product(broad_input.T, query_adapter_factor),
            adapter_scale * precise_product(query_middle.T, query_gradient),
            adapter_scale * precise_product(broad_input.T, value_adapter_factor),
            adapter_scale * precise_product(value_middle.T, value_gradient))
```

```python
import functools

import jax
import jax.numpy as jnp
from jax import lax
from jax.experimental import pallas as pl
from jax.experimental.pallas import tpu as pltpu
from jax.sharding import PartitionSpec as P

HQ = 128
KVH = 8
HD = 128
R = 32

adapter_scale = 2.0
mask_fill = -1e30
highest = lax.Precision.HIGHEST
MESH = pl.DeviceIdType.MESH
ROWS = 8


def contract_exact(left_side, right_side):
    return lax.dot_general(
        left_side,
        right_side,
        (((1,), (1,)), ((), ())),
        precision=highest,
        preferred_element_type=jnp.float32,
    )


def precise_product(left_side, right_side):
    return jnp.dot(left_side, right_side, precision=highest, preferred_element_type=jnp.float32)


def drain(ref, sem):
    pltpu.make_async_copy(ref, ref, sem).wait()


def send_to(src, dst, send_sem, recv_sem, device):
    return pltpu.make_async_remote_copy(
        src_ref=src,
        dst_ref=dst,
        send_sem=send_sem,
        recv_sem=recv_sem,
        device_id=device,
        device_id_type=MESH,
    )


def spread(count, me, device_of, src_of, dst, send_sem, recv_sem):
    pltpu.make_async_copy(src_of(me), dst, recv_sem).start()

    def step(offset, carry):
        peer = lax.rem(me + offset, count)
        send_to(src_of(peer), dst, send_sem, recv_sem, device_of(peer)).start()
        return carry

    lax.fori_loop(1, count, step, 0)


def greet(count, me, device_of):
    def step(offset, carry):
        peer = lax.rem(me + offset, count)
        pl.semaphore_signal(
            pltpu.get_barrier_semaphore(), inc=1, device_id=device_of(peer), device_id_type=MESH
        )
        return carry

    lax.fori_loop(1, count, step, 0)


def rows_of(index, count):
    return pl.ds(pl.multiple_of(index * count, count), count)


def grad_kernel(
    sizes,
    a_ref,
    w_ref,
    li_ref,
    dw_ref,
    out_ref,
    mid_ref,
    a_buf,
    w_buf,
    c_send,
    c_recv,
    mid_part,
    mid_recv,
    mid_sum,
    mid_all,
    first_sems,
    w_sems,
    x_sems,
    ring_send,
    ring_recv,
    c_sems,
    m_sems,
):
    gx, gy, gz = sizes
    col, lev, place = lax.axis_index("gx"), lax.axis_index("gy"), lax.axis_index("gz")
    far, core = place // 2, lax.rem(place, 2)
    slots = gy * gz
    slot_me = lev * gz + place
    pair_me = col * 2 + core
    seq, width = a_ref.shape
    chunk = seq // gy
    half = chunk // 2
    diagonal = col == lev

    def slot_device(index):
        return (col, index // gz, lax.rem(index, gz))

    def pair_device(index):
        return (index // 2, lev, far * 2 + lax.rem(index, 2))

    greet(slots, slot_me, slot_device)
    greet(2 * gx, pair_me, pair_device)

    def greet_first(index, carry):
        @pl.when(jnp.logical_not(jnp.logical_and(diagonal, index == pair_me)))
        def _():
            pl.semaphore_signal(
                pltpu.get_barrier_semaphore(),
                inc=1,
                device_id=(index // 2, col, far * 2 + lax.rem(index, 2)),
                device_id_type=MESH,
            )

        return carry

    lax.fori_loop(0, 2 * gx, greet_first, 0)
    extra = jnp.where(diagonal, 1, 0)
    pl.semaphore_wait(pltpu.get_barrier_semaphore(), slots - 1 + 4 * gx - 1 - extra)

    def first_send(index, carry):
        level = lax.rem(col + index // 2, gy)
        side = lax.rem(index, 2)
        source = a_ref.at[rows_of(level * 2 + side, half)]
        target = a_buf.at[level, far, core, rows_of(col, half)]
        mine = jnp.logical_and(diagonal, jnp.logical_and(level == lev, side == core))

        @pl.when(mine)
        def _():
            pltpu.make_async_copy(source, target, first_sems.at[1]).start()

        @pl.when(jnp.logical_not(mine))
        def _():
            send_to(
                source,
                target,
                first_sems.at[0],
                first_sems.at[1],
                (lev, level, far * 2 + side),
            ).start()

        return carry

    lax.fori_loop(0, 2 * gy, first_send, 0)

    sibling = (col, lev, far * 2 + 1 - core)
    opposite = (col, lev, (1 - far) * 2 + core)
    own_w = pltpu.make_async_copy(w_ref, w_buf.at[0], w_sems.at[0])
    own_w.start()
    twin_w = send_to(w_ref, w_buf.at[1], w_sems.at[1], w_sems.at[2], sibling)
    twin_w.start()

    packed = seq // 2
    mid_part[...] = jnp.dot(
        li_ref[:packed, :], dw_ref[0], preferred_element_type=jnp.float32
    ) + jnp.dot(li_ref[packed:, :], dw_ref[1], preferred_element_type=jnp.float32)
    piece = packed // slots
    spread(
        slots,
        slot_me,
        slot_device,
        lambda index: mid_part.at[rows_of(index, piece)],
        mid_recv.at[slot_me],
        m_sems.at[0],
        m_sems.at[1],
    )

    up = (col, lax.rem(lev + 1, gy), place)
    down = (col, lax.rem(lev + gy - 1, gy), place)

    def ring(way, index, slot, which):
        block = a_buf.at[slot, which]
        return send_to(
            block, block, ring_send.at[way, index], ring_recv.at[way, index], (up, down)[way]
        )

    def behind(hop):
        return lax.rem(lev + gy - hop, gy)

    def ahead(hop):
        return lax.rem(lev + hop, gy)

    def multiply(slot):
        def one_side(side, carry):
            total = jnp.zeros((gx * half, w_ref.shape[0]), jnp.float32)
            for which in range(2):
                for part in range(2):
                    start = (which * 2 + part) * width
                    total += lax.dot_general(
                        a_buf[slot, which, part],
                        w_buf[side, :, start : start + width],
                        (((1,), (1,)), ((), ())),
                        preferred_element_type=jnp.float32,
                    )
            c_send[slot * 2 + side] = total.astype(jnp.bfloat16)
            return carry

        lax.fori_loop(0, 2, one_side, 0)
        spread(
            2 * gx,
            pair_me,
            pair_device,
            lambda index: c_send.at[
                slot * 2 + lax.rem(lax.rem(index, 2) + core, 2), rows_of(index // 2, half)
            ],
            c_recv.at[col, rows_of(slot * 2 + core, half)],
            c_sems.at[0],
            c_sems.at[1],
        )

    drain(a_buf.at[lev, far], first_sems.at[1])
    ring(0, 0, lev, far).start()
    ring(1, 0, lev, far).start()
    cross = send_to(a_buf.at[lev, far], a_buf.at[lev, far], x_sems.at[0], x_sems.at[1], opposite)
    cross.start()
    cross.wait_recv()
    ring(0, 1, lev, 1 - far).start()
    ring(1, 1, lev, 1 - far).start()

    drain(mid_recv, m_sems.at[1])
    mid_sum[...] = jnp.sum(mid_recv[...], axis=0)
    spread(
        slots,
        slot_me,
        slot_device,
        lambda index: mid_sum,
        mid_all.at[rows_of(slot_me, piece)],
        m_sems.at[2],
        m_sems.at[3],
    )

    own_w.wait()
    twin_w.wait_recv()
    multiply(lev)
    last = gy // 2

    def hop_step(hop, carry):
        index = 2 * (hop - 1)
        ring(0, index, behind(hop), far).wait_recv()
        ring(0, index + 2, behind(hop), far).start()
        ring(1, index, ahead(hop), far).wait_recv()

        @pl.when(hop < last - 1)
        def _():
            ring(1, index + 2, ahead(hop), far).start()

        ring(0, index + 1, behind(hop), 1 - far).wait_recv()

        @pl.when(hop < last - 1)
        def _():
            ring(0, index + 3, behind(hop), 1 - far).start()

        ring(1, index + 1, ahead(hop), 1 - far).wait_recv()

        @pl.when(hop < last - 1)
        def _():
            ring(1, index + 3, ahead(hop), 1 - far).start()

        @pl.when(hop == last - 1)
        def _():
            ring(1, index + 2, ahead(hop), 1 - far).start()

        def two(way, inner):
            multiply(lax.rem(lev + gy + (2 * way - 1) * hop, gy))
            return inner

        lax.fori_loop(0, 2, two, 0)
        return carry

    lax.fori_loop(1, last, hop_step, 0)
    end = 2 * (last - 1)
    ring(0, end, behind(last), far).wait_recv()
    ring(1, end, ahead(last), 1 - far).wait_recv()
    multiply(ahead(last))

    twin_w.wait_send()
    cross.wait_send()
    for way in range(2):
        for index in range(end + 1):
            ring(way, index, lev, 0).wait_send()

    @pl.when(diagonal)
    def _():
        drain(a_buf.at[0, 0, 0], first_sems.at[0])
        drain(a_buf.at[0, 0, 1, : (gx - 1) * half], first_sems.at[0])

    @pl.when(jnp.logical_not(diagonal))
    def _():
        drain(a_buf.at[0, 0], first_sems.at[0])

    drain(mid_recv.at[: slots - 1], m_sems.at[0])
    drain(mid_recv.at[: slots - 1], m_sems.at[2])
    drain(mid_all, m_sems.at[3])
    mid_ref[...] = mid_all[...]
    drain(c_send.at[: 2 * gy - 1], c_sems.at[0])
    drain(c_recv, c_sems.at[1])

    def add_up(index, carry):
        rows = rows_of(index, half)
        total = c_recv[0, rows, :].astype(jnp.float32)
        for source in range(1, gx):
            total += c_recv[source, rows, :].astype(jnp.float32)
        out_ref[rows, :] = total.astype(jnp.bfloat16)
        return carry

    lax.fori_loop(0, seq // half, add_up, 0)


def grad_call(sizes, out_grad, out_weight, layer_input, down_pair):
    gx, gy, gz = sizes
    seq, width = out_grad.shape
    heads, depth = out_weight.shape
    half = seq // gy // 2
    slots = gy * gz
    piece = seq // 2 // slots
    vmem = pl.BlockSpec(memory_space=pltpu.VMEM)
    anywhere = pl.BlockSpec(memory_space=pl.ANY)
    low = jnp.bfloat16
    return pl.pallas_call(
        functools.partial(grad_kernel, sizes),
        out_shape=(
            jax.ShapeDtypeStruct((seq, heads), low),
            jax.ShapeDtypeStruct((seq // 2, 128), jnp.float32),
        ),
        in_specs=[anywhere, anywhere, vmem, vmem],
        out_specs=(vmem, vmem),
        scratch_shapes=[
            pltpu.VMEM((gy, 2, 2, gx * half, width), low),
            pltpu.VMEM((2, heads, depth), low),
            pltpu.VMEM((gy * 2, gx * half, heads), low),
            pltpu.VMEM((gx, seq, heads), low),
            pltpu.VMEM((seq // 2, 128), jnp.float32),
            pltpu.VMEM((slots, piece, 128), jnp.float32),
            pltpu.VMEM((piece, 128), jnp.float32),
            pltpu.VMEM((seq // 2, 128), jnp.float32),
            pltpu.SemaphoreType.DMA((2,)),
            pltpu.SemaphoreType.DMA((3,)),
            pltpu.SemaphoreType.DMA((2,)),
            pltpu.SemaphoreType.DMA((2, gy - 1)),
            pltpu.SemaphoreType.DMA((2, gy - 1)),
            pltpu.SemaphoreType.DMA((2,)),
            pltpu.SemaphoreType.DMA((4,)),
        ],
        compiler_params=pltpu.CompilerParams(
            collective_id=0, has_side_effects=True, vmem_limit_bytes=44 << 20
        ),
        cost_estimate=pl.CostEstimate(
            flops=2 * seq * heads * depth * gx, bytes_accessed=16 << 20, transcendentals=0
        ),
    )(out_grad, out_weight, layer_input, down_pair)


def sum_kernel(
    sizes,
    factor_ref,
    raise_ref,
    value_ref,
    li_ref,
    down_ref,
    raise_out,
    value_out,
    factor_recv,
    factor_sum,
    factor_all,
    raise_recv,
    raise_sum,
    raise_all,
    value_recv,
    value_sum,
    value_plane,
    value_done,
    value_level,
    value_all,
    down_part,
    down_recv,
    down_sum,
    down_all,
    sends,
    recvs,
):
    gx, gy, gz = sizes
    col, lev, place = lax.axis_index("gx"), lax.axis_index("gy"), lax.axis_index("gz")
    slots = gy * gz
    slot_me = lev * gz + place

    def slot_device(index):
        return (col, index // gz, lax.rem(index, gz))

    def column_device(index):
        return (index, lev, place)

    def level_device(index):
        return (col, index, place)

    def place_device(index):
        return (col, lev, index)

    greet(slots, slot_me, slot_device)
    greet(gx, col, column_device)
    pl.semaphore_wait(pltpu.get_barrier_semaphore(), slots + gx - 2)

    spread(slots, slot_me, slot_device, lambda i: factor_ref.at[i], factor_recv.at[slot_me], sends.at[0], recvs.at[0])
    spread(gx, col, column_device, lambda i: value_ref.at[i], value_recv.at[col], sends.at[1], recvs.at[1])
    spread(gx, col, column_device, lambda i: raise_ref.at[i], raise_recv.at[col], sends.at[2], recvs.at[2])

    drain(factor_recv, recvs.at[0])
    factor_sum[...] = jnp.sum(factor_recv[...], axis=0)
    spread(slots, slot_me, slot_device, lambda i: factor_sum, factor_all.at[slot_me], sends.at[3], recvs.at[3])
    drain(value_recv, recvs.at[1])
    value_sum[...] = jnp.sum(value_recv[...], axis=0)
    spread(gz, place, place_device, lambda i: value_sum, value_plane.at[place], sends.at[4], recvs.at[4])
    drain(raise_recv, recvs.at[2])
    raise_sum[...] = jnp.sum(raise_recv[...], axis=0)
    spread(gx, col, column_device, lambda i: raise_sum, raise_all.at[col], sends.at[5], recvs.at[5])

    packed = factor_ref.shape[0] * factor_ref.shape[1]
    drain(factor_all, recvs.at[3])
    factor = factor_all[...].reshape(packed, 128)
    factor_high = factor.astype(jnp.bfloat16)
    factor_low = (factor - factor_high.astype(jnp.float32)).astype(jnp.bfloat16)

    def project(rows):
        block = li_ref[rows, :]
        dims = (((0,), (0,)), ((), ()))
        return lax.dot_general(
            block, factor_high, dims, preferred_element_type=jnp.float32
        ) + lax.dot_general(block, factor_low, dims, preferred_element_type=jnp.float32)

    first = project(slice(0, packed))
    second = project(slice(packed, 2 * packed))
    lane = lax.broadcasted_iota(jnp.int32, first.shape, 1)
    down_part[...] = (adapter_scale * jnp.where(lane < 64, first, second)).reshape(down_part.shape)
    spread(gx, col, column_device, lambda i: down_part.at[i], down_recv.at[col], sends.at[6], recvs.at[6])

    drain(value_plane, recvs.at[4])
    value_done[...] = jnp.sum(value_plane[...], axis=0)
    spread(gy, lev, level_device, lambda i: value_done, value_level.at[lev], sends.at[7], recvs.at[7])
    drain(value_level, recvs.at[7])
    spread(gx, col, column_device, lambda i: value_level, value_all.at[col], sends.at[8], recvs.at[8])

    drain(down_recv, recvs.at[6])
    down_sum[...] = jnp.sum(down_recv[...], axis=0)
    spread(gx, col, column_device, lambda i: down_sum, down_all.at[col], sends.at[9], recvs.at[9])

    drain(raise_all, recvs.at[5])
    raise_out[...] = raise_all[...]
    drain(value_all, recvs.at[8])
    value_out[...] = value_all[...]
    drain(down_all, recvs.at[9])
    down_ref[...] = down_all[...]
    drain(factor_recv.at[: slots - 1], sends.at[0])
    drain(value_recv.at[: gx - 1], sends.at[1])
    drain(raise_recv.at[: gx - 1], sends.at[2])
    drain(factor_all.at[: slots - 1], sends.at[3])
    drain(value_plane.at[: gz - 1], sends.at[4])
    drain(raise_all.at[: gx - 1], sends.at[5])
    drain(down_recv.at[: gx - 1], sends.at[6])
    drain(value_level.at[: gy - 1], sends.at[7])
    drain(value_all.at[: gx - 1], sends.at[8])
    drain(down_all.at[: gx - 1], sends.at[9])


def sum_call(sizes, factor, raised, value, layer_input):
    gx, gy, gz = sizes
    slots = gy * gz
    width = layer_input.shape[1]
    vmem = pl.BlockSpec(memory_space=pltpu.VMEM)
    single = jnp.float32
    down_shape = (gx, width // gx, 128)
    return pl.pallas_call(
        functools.partial(sum_kernel, sizes),
        out_shape=(
            jax.ShapeDtypeStruct(down_shape, single),
            jax.ShapeDtypeStruct(raised.shape, single),
            jax.ShapeDtypeStruct((gx, gy) + value.shape[1:], single),
        ),
        in_specs=[vmem] * 4,
        out_specs=(vmem,) * 3,
        scratch_shapes=[
            pltpu.VMEM(factor.shape, single),
            pltpu.VMEM(factor.shape[1:], single),
            pltpu.VMEM(factor.shape, single),
            pltpu.VMEM(raised.shape, single),
            pltpu.VMEM(raised.shape[1:], single),
            pltpu.VMEM(raised.shape, single),
            pltpu.VMEM(value.shape, single),
            pltpu.VMEM(value.shape[1:], single),
            pltpu.VMEM((gz,) + value.shape[1:], single),
            pltpu.VMEM(value.shape[1:], single),
            pltpu.VMEM((gy,) + value.shape[1:], single),
            pltpu.VMEM((gx, gy) + value.shape[1:], single),
            pltpu.VMEM(down_shape, single),
            pltpu.VMEM(down_shape, single),
            pltpu.VMEM(down_shape[1:], single),
            pltpu.VMEM(down_shape, single),
            pltpu.SemaphoreType.DMA((10,)),
            pltpu.SemaphoreType.DMA((10,)),
        ],
        compiler_params=pltpu.CompilerParams(
            collective_id=1, has_side_effects=True, vmem_limit_bytes=24 << 20
        ),
    )(factor, raised, value, layer_input)


def pack_halves(array):
    rows = array.shape[0] // 2
    return jnp.concatenate([array[:rows], array[rows:]], axis=1)


def down_pair_of(query_down, value_down):
    pair = jnp.concatenate([query_down, value_down], axis=1)
    none = jnp.zeros_like(pair)
    return jnp.stack(
        [jnp.concatenate([pair, none], axis=1), jnp.concatenate([none, pair], axis=1)]
    )


def finish(sizes, factor_part, raise_part, value_part, layer_input):
    gx, gy, gz = sizes
    slots = gy * gz
    width = raise_part.shape[1]
    factor = pack_halves(factor_part).reshape(slots, -1, 128)
    raised = jnp.concatenate(
        [raise_part[:, at : at + 128] for at in range(0, width, 128)], axis=0
    ).reshape(gx, -1, 128)
    per = R // gx
    value = jnp.pad(value_part.reshape(gx, per, HD), ((0, 0), (0, ROWS - per), (0, 0)))
    down, raise_sum, value_sum = sum_call(sizes, factor, raised, value, layer_input)
    down = down.reshape(-1, 128)
    down = down[:, :64] + down[:, 64:]
    raise_sum = raise_sum.reshape(-1, 128)
    query_up_grad = jnp.concatenate(
        [raise_sum[at : at + R] for at in range(0, raise_sum.shape[0], R)], axis=1
    )
    value_up_grad = value_sum[:, :, :per].transpose(0, 2, 1, 3).reshape(R, gy * HD)
    return (down[:, :R], query_up_grad, down[:, R:], value_up_grad)


def body(
    sizes,
    out_grad,
    layer_input,
    out_weight,
    saved_queries,
    saved_keys,
    saved_values,
    query_down,
    query_up,
    value_down,
    value_up,
    lengths,
):
    seq_rows = out_grad.shape[0]
    head_count = saved_queries.shape[1] // HD
    group_size = HQ // KVH
    slot_index = lax.axis_index(("gy", "gz"))
    kv_start = slot_index * head_count // group_size * HD
    attn_full, middle = grad_call(
        sizes, out_grad, out_weight, layer_input, down_pair_of(query_down, value_down)
    )
    down_total = jnp.concatenate([middle[:, :64], middle[:, 64:]], axis=0)
    position = jnp.arange(seq_rows)
    valid_rows = position < lengths[0]
    attn_grad = jnp.where(valid_rows[:, None], attn_full, jnp.zeros_like(attn_full))
    visible = (position[None, :] <= position[:, None]) & valid_rows[None, :]
    head_keys = lax.dynamic_slice_in_dim(saved_keys, kv_start, HD, 1)
    head_values = lax.dynamic_slice_in_dim(saved_values, kv_start, HD, 1)
    score_scale = HD ** (-0.5)
    query_heads = saved_queries.reshape(seq_rows, head_count, HD)
    grad_heads = attn_grad.reshape(seq_rows, head_count, HD)
    scores = (
        jnp.einsum("qhd,kd->hqk", query_heads, head_keys, preferred_element_type=jnp.float32)
        * score_scale
    )
    scores = jnp.where(visible[None], scores, mask_fill)
    largest = jnp.max(scores, axis=-1, keepdims=True)
    raised = jnp.exp(scores - largest)
    attention = raised / jnp.sum(raised, axis=-1, keepdims=True)
    attention_low = attention.astype(jnp.bfloat16)
    value_gradient = jnp.einsum(
        "hqk,qhd->kd", attention_low, grad_heads, preferred_element_type=jnp.float32
    )
    prob_grad = jnp.einsum(
        "qhd,kd->hqk", grad_heads, head_values, preferred_element_type=jnp.float32
    )
    centre = jnp.sum(attention * prob_grad, axis=-1, keepdims=True)
    score_grad = (attention * (prob_grad - centre)).astype(jnp.bfloat16)
    query_gradient = (
        jnp.einsum("hqk,kd->qhd", score_grad, head_keys, preferred_element_type=jnp.float32)
        * score_scale
    )
    query_gradient = query_gradient.reshape(seq_rows, head_count * HD)
    up_local = query_up.astype(jnp.float32)
    query_middle = down_total[:, :R]
    value_middle = down_total[:, R:]
    value_up_head = lax.dynamic_slice_in_dim(value_up, kv_start, HD, 1).astype(jnp.float32)
    factor_part = jnp.concatenate(
        [contract_exact(query_gradient, up_local), contract_exact(value_gradient, value_up_head)],
        axis=1,
    )
    value_part = adapter_scale * precise_product(value_middle.T, value_gradient)
    raise_part = adapter_scale * precise_product(query_middle.T, query_gradient)
    return finish(sizes, factor_part, raise_part, value_part, layer_input)


def solution(mesh):
    sizes = tuple(mesh.shape[name] for name in ("gx", "gy", "gz"))
    return jax.shard_map(
        functools.partial(body, sizes),
        mesh=mesh,
        in_specs=(
            P("gx", ("gy", "gz")),
            P("gx", ("gy", "gz")),
            P(("gy", "gz"), "gx"),
            P("gx", ("gy", "gz")),
            P("gx", None),
            P("gx", None),
            P(("gy", "gz"), None),
            P(None, ("gy", "gz")),
            P(("gy", "gz"), None),
            P(),
            P("gx"),
        ),
        out_specs=(P(("gy", "gz"), None), P(None, ("gy", "gz")), P(("gy", "gz"), None), P()),
        check_vma=False,
    )
```

```python
import functools

import jax
import jax.numpy as jnp
from jax import lax
from jax.experimental import pallas as pl
from jax.experimental.pallas import tpu as pltpu
from jax.sharding import PartitionSpec as P

HQ = 128
KVH = 8
HD = 128
R = 32

adapter_scale = 2.0
mask_fill = -1e30
highest = lax.Precision.HIGHEST
MESH = pl.DeviceIdType.MESH
ROWS = 8


def contract_exact(left_side, right_side):
    return lax.dot_general(
        left_side,
        right_side,
        (((1,), (1,)), ((), ())),
        precision=highest,
        preferred_element_type=jnp.float32,
    )


def precise_product(left_side, right_side):
    return jnp.dot(left_side, right_side, precision=highest, preferred_element_type=jnp.float32)


def drain(ref, sem):
    pltpu.make_async_copy(ref, ref, sem).wait()


def send_to(src, dst, send_sem, recv_sem, device):
    return pltpu.make_async_remote_copy(
        src_ref=src,
        dst_ref=dst,
        send_sem=send_sem,
        recv_sem=recv_sem,
        device_id=device,
        device_id_type=MESH,
    )


def spread(count, me, device_of, src_of, dst, send_sem, recv_sem):
    pltpu.make_async_copy(src_of(me), dst, recv_sem).start()

    def step(offset, carry):
        peer = lax.rem(me + offset, count)
        send_to(src_of(peer), dst, send_sem, recv_sem, device_of(peer)).start()
        return carry

    lax.fori_loop(1, count, step, 0)


def greet(count, me, device_of):
    def step(offset, carry):
        peer = lax.rem(me + offset, count)
        pl.semaphore_signal(
            pltpu.get_barrier_semaphore(), inc=1, device_id=device_of(peer), device_id_type=MESH
        )
        return carry

    lax.fori_loop(1, count, step, 0)


def rows_of(index, count):
    return pl.ds(pl.multiple_of(index * count, count), count)


def grad_kernel(
    sizes,
    a_ref,
    w_ref,
    li_ref,
    dw_ref,
    out_ref,
    mid_ref,
    t_buf,
    a_buf,
    w_buf,
    c_part,
    c_own,
    c_recv,
    x_send,
    d_recv,
    mid_part,
    mid_recv,
    mid_sum,
    mid_all,
    t_sems,
    first_sems,
    w_sems,
    far_sems,
    twin_sems,
    ring_send,
    ring_recv,
    c_sems,
    c_arrived,
    d_sems,
    m_sems,
    gate,
):
    gx, gy, gz = sizes
    col, lev, place = lax.axis_index("gx"), lax.axis_index("gy"), lax.axis_index("gz")
    far, core = place // 2, lax.rem(place, 2)
    sides = gx // 2
    near_x, side = col // sides, lax.rem(col, sides)
    slots = gy * gz
    slot_me = lev * gz + place
    seq, width = a_ref.shape
    heads = w_ref.shape[0]
    unit = seq // slots
    chunk = unit * gz
    last = gy // 2

    def slot_device(index):
        return (col, index // gz, lax.rem(index, gz))

    def plane_device(index):
        return (index // gz, lev, lax.rem(index, gz))

    greet(slots, slot_me, slot_device)
    greet(gx * gz, col * gz + place, plane_device)

    packed = seq // 2
    mid_part[...] = jnp.dot(
        li_ref[:packed, :], dw_ref[0], preferred_element_type=jnp.float32
    ) + jnp.dot(li_ref[packed:, :], dw_ref[1], preferred_element_type=jnp.float32)

    pl.semaphore_wait(pltpu.get_barrier_semaphore(), slots - 1 + gx * gz - 1)

    def level_send(away):
        other = lax.rem(lev + away, gy)
        return send_to(
            a_ref.at[rows_of(other, chunk)],
            t_buf.at[lev],
            t_sems.at[0, away],
            t_sems.at[1, away],
            (col, other, place),
        )

    order = [1, gy - 1]
    for away in range(2, last):
        order += [away, gy - away]
    order.append(last)
    for away in order:
        level_send(away).start()

    def column_send(to, block):
        def one(index, carry):
            at = lax.rem(place + index, gz)
            source = block.at[rows_of(at, unit)]
            target = a_buf.at[place, 0, rows_of(side * 2 + near_x, unit)]
            mine = jnp.logical_and(col == to, at == place)

            @pl.when(mine)
            def _():
                pltpu.make_async_copy(source, target, first_sems.at[1]).start()

            @pl.when(jnp.logical_not(mine))
            def _():
                send_to(
                    source, target, first_sems.at[0], first_sems.at[1], (to, lev, at)
                ).start()

            return carry

        lax.fori_loop(0, gz, one, 0)

    column_send(lev, a_ref.at[rows_of(lev, chunk)])

    sibling = (col, lev, far * 2 + 1 - core)
    opposite = (col, lev, (1 - far) * 2 + core)
    band = heads // 2
    own_w = pltpu.make_async_copy(w_ref, w_buf.at[0], w_sems.at[0])
    own_w.start()
    twin_w = send_to(w_ref, w_buf.at[1], w_sems.at[1], w_sems.at[2], sibling)
    twin_w.start()

    def far_w(piece):
        rows = (pl.ds(0, band // 2), pl.ds(band // 2, band // 2), pl.ds(band, band))[piece]
        return send_to(
            w_ref.at[rows], w_buf.at[2, rows], far_sems.at[0, piece], far_sems.at[1, piece], opposite
        )

    def pass_w(part):
        rows = pl.ds(part * band, band)
        return send_to(
            w_buf.at[2, rows],
            w_buf.at[3, rows],
            twin_sems.at[0, part],
            twin_sems.at[1, part],
            sibling,
        )

    far_w(0).start()

    for away in order:
        other = lax.rem(lev + gy - away, gy)
        level_send(away).wait_recv()
        column_send(other, t_buf.at[other])

    up = (col, lax.rem(lev + 1, gy), place)
    down = (col, lax.rem(lev + gy - 1, gy), place)

    def ring(way, hop, which):
        parts = slice(2 * which, 2 * which + 2)
        start = 2 * hop - 3 + way if hop > 1 else 0
        end = 2 * hop - 1 + (way if hop < last else 0)
        index = 2 * (hop - 1) + (which if hop < last else 0)
        return send_to(
            a_buf.at[parts, start],
            a_buf.at[parts, end],
            ring_send.at[way, index],
            ring_recv.at[way, index],
            (up, down)[way],
        )

    def multiply(start, steps, base, first, count, runs):
        columns = slice(first, first + count)

        def one_block(index, carry):
            block = base + index
            total = jnp.zeros((steps * gx * unit, count), jnp.float32)
            for part in range(gz):
                total += lax.dot_general(
                    a_buf[part, start : start + steps].reshape(steps * gx * unit, width),
                    w_buf[block, first : first + count, part * width : (part + 1) * width],
                    (((1,), (1,)), ((), ())),
                    preferred_element_type=jnp.float32,
                )
            total = total.reshape(steps, sides, 2, unit, count)
            c_part[block, start : start + steps, :, :, :, columns] = total.astype(jnp.bfloat16)
            for way in range(sides):

                @pl.when(side == way)
                def _():
                    c_own[block, start : start + steps, :, :, columns] = total[:, way]

            for at, length, group in runs:
                for away in range(1, sides):
                    other = lax.rem(side + away, sides)
                    send_to(
                        c_part.at[block, at : at + length, other, :, :, columns],
                        c_recv.at[away - 1, block, at : at + length, :, :, columns],
                        c_sems.at[0],
                        c_arrived.at[group],
                        (near_x * sides + other, lev, place),
                    ).start()
            return carry

        lax.fori_loop(0, 2, one_block, 0)

    cut = gy - 2

    def runs_of(start, steps):
        return [
            (at, length, group)
            for at, length, group in (
                (start, min(start + steps, cut) - start, 0),
                (max(start, cut), start + steps - max(start, cut), 1),
            )
            if length > 0
        ]

    def near(start, steps):
        multiply(start, steps, 0, 0, heads, runs_of(start, steps))

    def far_part(start, part):
        multiply(start, 2, 2, part * band, band, runs_of(start, 2))

    drain(a_buf.at[: gz - 1, 0], first_sems.at[0])
    drain(a_buf.at[gz - 1, 0, : (gx - 1) * unit], first_sems.at[0])

    def gate_signal(offset, carry):
        peer = lax.rem(near_x * gz + place + offset, 2 * gz)
        pl.semaphore_signal(
            gate,
            inc=1,
            device_id=(peer // gz * sides + side, lev, lax.rem(peer, gz)),
            device_id_type=MESH,
        )
        return carry

    lax.fori_loop(1, 2 * gz, gate_signal, 0)
    drain(a_buf.at[:, 0], first_sems.at[1])
    for which in range(2):
        for way in range(2):
            ring(way, 1, which).start()
    piece = packed // slots
    spread(
        slots,
        slot_me,
        slot_device,
        lambda index: mid_part.at[rows_of(index, piece)],
        mid_recv.at[slot_me],
        m_sems.at[0],
        m_sems.at[1],
    )

    pl.semaphore_wait(gate, 2 * gz - 1)
    far_w(1).start()
    far_w(2).start()
    own_w.wait()
    twin_w.wait_recv()
    near(0, 1)
    for hop in range(1, last):
        for which in range(2):
            for way in range(2):
                ring(way, hop, which).wait_recv()
                if hop < last - 1 or way == which:
                    ring(way, hop + 1, which).start()
        near(2 * hop - 1, 2)
        if hop == 1:
            far_w(0).wait_recv()
            far_w(1).wait_recv()
            pass_w(0).start()
        if hop == last - 2:
            pass_w(0).wait_recv()
            for start in range(0, 2 * hop, 2):
                far_part(start, 0)
        if hop == last - 1:
            if last == 2:
                pass_w(0).wait_recv()
            far_part(2 * hop - 2, 0)
            far_w(2).wait_recv()
            pass_w(1).start()
            pass_w(1).wait_recv()
            for start in range(0, 2 * hop, 2):
                far_part(start, 1)
    ring(0, last, 0).wait_recv()
    ring(1, last, 1).wait_recv()
    near(gy - 1, 1)
    far_part(gy - 2, 0)
    far_part(gy - 2, 1)

    def hand_on(start, end, group):
        drain(c_recv.at[:, :, start:end], c_arrived.at[group])

        def one(block, carry):
            total = c_own[block, start:end]
            for away in range(sides - 1):
                total += c_recv[away, block, start:end].astype(jnp.float32)
            x_send[block, start:end] = total.astype(jnp.bfloat16)
            return carry

        lax.fori_loop(0, gz, one, 0)
        target = d_recv.at[near_x, place, start:end]
        for block in range(gz):
            at = (far if block < 2 else 1 - far) * 2 + (1 - core if block % 2 else core)
            for turn in range(2):
                half = lax.rem(near_x + turn, 2)
                source = x_send.at[block, start:end, half]
                if block == 0 and turn == 0:
                    pltpu.make_async_copy(source, target, d_sems.at[1]).start()
                else:
                    send_to(
                        source, target, d_sems.at[0], d_sems.at[1], (half * sides + side, lev, at)
                    ).start()

    drain(mid_recv, m_sems.at[1])
    mid_sum[...] = jnp.sum(mid_recv[...], axis=0)
    spread(
        slots,
        slot_me,
        slot_device,
        lambda index: mid_sum,
        mid_all.at[rows_of(slot_me, piece)],
        m_sems.at[2],
        m_sems.at[3],
    )
    hand_on(0, cut, 0)
    hand_on(cut, gy, 1)

    for away in order:
        level_send(away).wait_send()
    twin_w.wait_send()
    for part in range(3):
        far_w(part).wait_send()
    for part in range(2):
        pass_w(part).wait_send()
    for hop in range(1, last + 1):
        for which in range(2):
            for way in range(2):
                if hop < last or way == which:
                    ring(way, hop, which).wait_send()
    drain(mid_recv.at[: slots - 1], m_sems.at[0])
    drain(mid_recv.at[: slots - 1], m_sems.at[2])
    drain(mid_all, m_sems.at[3])
    mid_ref[...] = mid_all[...]
    drain(c_part.at[:, : gy * (sides - 1) // sides], c_sems.at[0])
    drain(x_send.at[:, :, 0], d_sems.at[0])
    drain(x_send.at[: gz - 1, :, 1], d_sems.at[0])
    drain(d_recv, d_sems.at[1])

    for start in range(gy):
        hop = (start + 1) // 2
        level = lax.rem(lev + (gy - hop if start % 2 else hop), gy)

        def one_place(at, carry):
            total = d_recv[0, at, start].astype(jnp.float32) + d_recv[1, at, start].astype(
                jnp.float32
            )
            out_ref[rows_of(level * gz + at, unit), :] = total.astype(jnp.bfloat16)
            return carry

        lax.fori_loop(0, gz, one_place, 0)


def grad_call(sizes, out_grad, out_weight, layer_input, down_pair):
    gx, gy, gz = sizes
    seq, width = out_grad.shape
    heads, depth = out_weight.shape
    slots = gy * gz
    unit = seq // slots
    piece = seq // 2 // slots
    sides = gx // 2
    vmem = pl.BlockSpec(memory_space=pltpu.VMEM)
    anywhere = pl.BlockSpec(memory_space=pl.ANY)
    low = jnp.bfloat16
    return pl.pallas_call(
        functools.partial(grad_kernel, sizes),
        out_shape=(
            jax.ShapeDtypeStruct((seq, heads), low),
            jax.ShapeDtypeStruct((seq // 2, 128), jnp.float32),
        ),
        in_specs=[anywhere, anywhere, vmem, vmem],
        out_specs=(vmem, vmem),
        scratch_shapes=[
            pltpu.VMEM((gy, unit * gz, width), low),
            pltpu.VMEM((gz, gy, gx * unit, width), low),
            pltpu.VMEM((gz, heads, depth), low),
            pltpu.VMEM((gz, gy, sides, 2, unit, heads), low),
            pltpu.VMEM((gz, gy, 2, unit, heads), jnp.float32),
            pltpu.VMEM((sides - 1, gz, gy, 2, unit, heads), low),
            pltpu.VMEM((gz, gy, 2, unit, heads), low),
            pltpu.VMEM((2, gz, gy, unit, heads), low),
            pltpu.VMEM((seq // 2, 128), jnp.float32),
            pltpu.VMEM((slots, piece, 128), jnp.float32),
            pltpu.VMEM((piece, 128), jnp.float32),
            pltpu.VMEM((seq // 2, 128), jnp.float32),
            pltpu.SemaphoreType.DMA((2, gy)),
            pltpu.SemaphoreType.DMA((2,)),
            pltpu.SemaphoreType.DMA((3,)),
            pltpu.SemaphoreType.DMA((2, 3)),
            pltpu.SemaphoreType.DMA((2, 2)),
            pltpu.SemaphoreType.DMA((2, gy - 1)),
            pltpu.SemaphoreType.DMA((2, gy - 1)),
            pltpu.SemaphoreType.DMA((1,)),
            pltpu.SemaphoreType.DMA((2,)),
            pltpu.SemaphoreType.DMA((2,)),
            pltpu.SemaphoreType.DMA((4,)),
            pltpu.SemaphoreType.REGULAR,
        ],
        compiler_params=pltpu.CompilerParams(
            collective_id=0, has_side_effects=True, vmem_limit_bytes=44 << 20
        ),
        cost_estimate=pl.CostEstimate(
            flops=2 * seq * heads * depth * gx, bytes_accessed=16 << 20, transcendentals=0
        ),
    )(out_grad, out_weight, layer_input, down_pair)


def sum_kernel(
    sizes,
    factor_ref,
    raise_ref,
    value_ref,
    li_ref,
    down_ref,
    raise_out,
    value_out,
    factor_recv,
    factor_sum,
    factor_all,
    raise_recv,
    raise_sum,
    raise_all,
    value_recv,
    value_sum,
    value_plane,
    value_done,
    value_level,
    value_all,
    down_part,
    down_recv,
    down_sum,
    down_all,
    sends,
    recvs,
):
    gx, gy, gz = sizes
    col, lev, place = lax.axis_index("gx"), lax.axis_index("gy"), lax.axis_index("gz")
    slots = gy * gz
    slot_me = lev * gz + place

    def slot_device(index):
        return (col, index // gz, lax.rem(index, gz))

    def column_device(index):
        return (index, lev, place)

    def level_device(index):
        return (col, index, place)

    def place_device(index):
        return (col, lev, index)

    greet(slots, slot_me, slot_device)
    greet(gx, col, column_device)
    pl.semaphore_wait(pltpu.get_barrier_semaphore(), slots + gx - 2)

    spread(slots, slot_me, slot_device, lambda i: factor_ref.at[i], factor_recv.at[slot_me], sends.at[0], recvs.at[0])
    spread(gx, col, column_device, lambda i: value_ref.at[i], value_recv.at[col], sends.at[1], recvs.at[1])
    spread(gx, col, column_device, lambda i: raise_ref.at[i], raise_recv.at[col], sends.at[2], recvs.at[2])

    drain(factor_recv, recvs.at[0])
    factor_sum[...] = jnp.sum(factor_recv[...], axis=0)
    spread(slots, slot_me, slot_device, lambda i: factor_sum, factor_all.at[slot_me], sends.at[3], recvs.at[3])
    drain(value_recv, recvs.at[1])
    value_sum[...] = jnp.sum(value_recv[...], axis=0)
    spread(gz, place, place_device, lambda i: value_sum, value_plane.at[place], sends.at[4], recvs.at[4])
    drain(raise_recv, recvs.at[2])
    raise_sum[...] = jnp.sum(raise_recv[...], axis=0)
    spread(gx, col, column_device, lambda i: raise_sum, raise_all.at[col], sends.at[5], recvs.at[5])

    packed = factor_ref.shape[0] * factor_ref.shape[1]
    drain(factor_all, recvs.at[3])
    factor = factor_all[...].reshape(packed, 128)
    factor_high = factor.astype(jnp.bfloat16)
    factor_low = (factor - factor_high.astype(jnp.float32)).astype(jnp.bfloat16)

    def project(rows):
        block = li_ref[rows, :]
        dims = (((0,), (0,)), ((), ()))
        return lax.dot_general(
            block, factor_high, dims, preferred_element_type=jnp.float32
        ) + lax.dot_general(block, factor_low, dims, preferred_element_type=jnp.float32)

    first = project(slice(0, packed))
    second = project(slice(packed, 2 * packed))
    lane = lax.broadcasted_iota(jnp.int32, first.shape, 1)
    down_part[...] = (adapter_scale * jnp.where(lane < 64, first, second)).reshape(down_part.shape)
    spread(gx, col, column_device, lambda i: down_part.at[i], down_recv.at[col], sends.at[6], recvs.at[6])

    drain(value_plane, recvs.at[4])
    value_done[...] = jnp.sum(value_plane[...], axis=0)
    spread(gy, lev, level_device, lambda i: value_done, value_level.at[lev], sends.at[7], recvs.at[7])
    drain(value_level, recvs.at[7])
    spread(gx, col, column_device, lambda i: value_level, value_all.at[col], sends.at[8], recvs.at[8])

    drain(down_recv, recvs.at[6])
    down_sum[...] = jnp.sum(down_recv[...], axis=0)
    spread(gx, col, column_device, lambda i: down_sum, down_all.at[col], sends.at[9], recvs.at[9])

    drain(raise_all, recvs.at[5])
    raise_out[...] = raise_all[...]
    drain(value_all, recvs.at[8])
    value_out[...] = value_all[...]
    drain(down_all, recvs.at[9])
    down_ref[...] = down_all[...]
    drain(factor_recv.at[: slots - 1], sends.at[0])
    drain(value_recv.at[: gx - 1], sends.at[1])
    drain(raise_recv.at[: gx - 1], sends.at[2])
    drain(factor_all.at[: slots - 1], sends.at[3])
    drain(value_plane.at[: gz - 1], sends.at[4])
    drain(raise_all.at[: gx - 1], sends.at[5])
    drain(down_recv.at[: gx - 1], sends.at[6])
    drain(value_level.at[: gy - 1], sends.at[7])
    drain(value_all.at[: gx - 1], sends.at[8])
    drain(down_all.at[: gx - 1], sends.at[9])


def sum_call(sizes, factor, raised, value, layer_input):
    gx, gy, gz = sizes
    slots = gy * gz
    width = layer_input.shape[1]
    vmem = pl.BlockSpec(memory_space=pltpu.VMEM)
    single = jnp.float32
    down_shape = (gx, width // gx, 128)
    return pl.pallas_call(
        functools.partial(sum_kernel, sizes),
        out_shape=(
            jax.ShapeDtypeStruct(down_shape, single),
            jax.ShapeDtypeStruct(raised.shape, single),
            jax.ShapeDtypeStruct((gx, gy) + value.shape[1:], single),
        ),
        in_specs=[vmem] * 4,
        out_specs=(vmem,) * 3,
        scratch_shapes=[
            pltpu.VMEM(factor.shape, single),
            pltpu.VMEM(factor.shape[1:], single),
            pltpu.VMEM(factor.shape, single),
            pltpu.VMEM(raised.shape, single),
            pltpu.VMEM(raised.shape[1:], single),
            pltpu.VMEM(raised.shape, single),
            pltpu.VMEM(value.shape, single),
            pltpu.VMEM(value.shape[1:], single),
            pltpu.VMEM((gz,) + value.shape[1:], single),
            pltpu.VMEM(value.shape[1:], single),
            pltpu.VMEM((gy,) + value.shape[1:], single),
            pltpu.VMEM((gx, gy) + value.shape[1:], single),
            pltpu.VMEM(down_shape, single),
            pltpu.VMEM(down_shape, single),
            pltpu.VMEM(down_shape[1:], single),
            pltpu.VMEM(down_shape, single),
            pltpu.SemaphoreType.DMA((10,)),
            pltpu.SemaphoreType.DMA((10,)),
        ],
        compiler_params=pltpu.CompilerParams(
            collective_id=1, has_side_effects=True, vmem_limit_bytes=24 << 20
        ),
    )(factor, raised, value, layer_input)


def pack_halves(array):
    rows = array.shape[0] // 2
    return jnp.concatenate([array[:rows], array[rows:]], axis=1)


def down_pair_of(query_down, value_down):
    pair = jnp.concatenate([query_down, value_down], axis=1)
    none = jnp.zeros_like(pair)
    return jnp.stack(
        [jnp.concatenate([pair, none], axis=1), jnp.concatenate([none, pair], axis=1)]
    )


def finish(sizes, factor_part, raise_part, value_part, layer_input):
    gx, gy, gz = sizes
    slots = gy * gz
    width = raise_part.shape[1]
    factor = pack_halves(factor_part).reshape(slots, -1, 128)
    raised = jnp.concatenate(
        [raise_part[:, at : at + 128] for at in range(0, width, 128)], axis=0
    ).reshape(gx, -1, 128)
    per = R // gx
    value = jnp.pad(value_part.reshape(gx, per, HD), ((0, 0), (0, ROWS - per), (0, 0)))
    down, raise_sum, value_sum = sum_call(sizes, factor, raised, value, layer_input)
    down = down.reshape(-1, 128)
    down = down[:, :64] + down[:, 64:]
    raise_sum = raise_sum.reshape(-1, 128)
    query_up_grad = jnp.concatenate(
        [raise_sum[at : at + R] for at in range(0, raise_sum.shape[0], R)], axis=1
    )
    value_up_grad = value_sum[:, :, :per].transpose(0, 2, 1, 3).reshape(R, gy * HD)
    return (down[:, :R], query_up_grad, down[:, R:], value_up_grad)


def body(
    sizes,
    out_grad,
    layer_input,
    out_weight,
    saved_queries,
    saved_keys,
    saved_values,
    query_down,
    query_up,
    value_down,
    value_up,
    lengths,
):
    seq_rows = out_grad.shape[0]
    head_count = saved_queries.shape[1] // HD
    group_size = HQ // KVH
    slot_index = lax.axis_index(("gy", "gz"))
    kv_start = slot_index * head_count // group_size * HD
    attn_full, middle = grad_call(
        sizes, out_grad, out_weight, layer_input, down_pair_of(query_down, value_down)
    )
    down_total = jnp.concatenate([middle[:, :64], middle[:, 64:]], axis=0)
    position = jnp.arange(seq_rows)
    valid_rows = position < lengths[0]
    attn_grad = jnp.where(valid_rows[:, None], attn_full, jnp.zeros_like(attn_full))
    visible = (position[None, :] <= position[:, None]) & valid_rows[None, :]
    head_keys = lax.dynamic_slice_in_dim(saved_keys, kv_start, HD, 1)
    head_values = lax.dynamic_slice_in_dim(saved_values, kv_start, HD, 1)
    score_scale = HD ** (-0.5)
    query_heads = saved_queries.reshape(seq_rows, head_count, HD)
    grad_heads = attn_grad.reshape(seq_rows, head_count, HD)
    scores = (
        jnp.einsum("qhd,kd->hqk", query_heads, head_keys, preferred_element_type=jnp.float32)
        * score_scale
    )
    scores = jnp.where(visible[None], scores, mask_fill)
    largest = jnp.max(scores, axis=-1, keepdims=True)
    raised = jnp.exp(scores - largest)
    attention = raised / jnp.sum(raised, axis=-1, keepdims=True)
    attention_low = attention.astype(jnp.bfloat16)
    value_gradient = jnp.einsum(
        "hqk,qhd->kd", attention_low, grad_heads, preferred_element_type=jnp.float32
    )
    prob_grad = jnp.einsum(
        "qhd,kd->hqk", grad_heads, head_values, preferred_element_type=jnp.float32
    )
    centre = jnp.sum(attention * prob_grad, axis=-1, keepdims=True)
    score_grad = (attention * (prob_grad - centre)).astype(jnp.bfloat16)
    query_gradient = (
        jnp.einsum("hqk,kd->qhd", score_grad, head_keys, preferred_element_type=jnp.float32)
        * score_scale
    )
    query_gradient = query_gradient.reshape(seq_rows, head_count * HD)
    up_local = query_up.astype(jnp.float32)
    query_middle = down_total[:, :R]
    value_middle = down_total[:, R:]
    value_up_head = lax.dynamic_slice_in_dim(value_up, kv_start, HD, 1).astype(jnp.float32)
    factor_part = jnp.concatenate(
        [contract_exact(query_gradient, up_local), contract_exact(value_gradient, value_up_head)],
        axis=1,
    )
    value_part = adapter_scale * precise_product(value_middle.T, value_gradient)
    raise_part = adapter_scale * precise_product(query_middle.T, query_gradient)
    return finish(sizes, factor_part, raise_part, value_part, layer_input)


def solution(mesh):
    sizes = tuple(mesh.shape[name] for name in ("gx", "gy", "gz"))
    return jax.shard_map(
        functools.partial(body, sizes),
        mesh=mesh,
        in_specs=(
            P("gx", ("gy", "gz")),
            P("gx", ("gy", "gz")),
            P(("gy", "gz"), "gx"),
            P("gx", ("gy", "gz")),
            P("gx", None),
            P("gx", None),
            P(("gy", "gz"), None),
            P(None, ("gy", "gz")),
            P(("gy", "gz"), None),
            P(),
            P("gx"),
        ),
        out_specs=(P(("gy", "gz"), None), P(None, ("gy", "gz")), P(("gy", "gz"), None), P()),
        check_vma=False,
    )
```

```python
import functools

import jax
import jax.numpy as jnp
from jax import lax
from jax.experimental import pallas as pl
from jax.experimental.pallas import tpu as pltpu
from jax.sharding import PartitionSpec as P

HQ = 128
KVH = 8
HD = 128
R = 32

adapter_scale = 2.0
mask_fill = -1e30
MESH = pl.DeviceIdType.MESH
ROWS = 8


def drain(ref, sem):
    pltpu.make_async_copy(ref, ref, sem).wait()


def send_to(src, dst, send_sem, recv_sem, device):
    return pltpu.make_async_remote_copy(
        src_ref=src,
        dst_ref=dst,
        send_sem=send_sem,
        recv_sem=recv_sem,
        device_id=device,
        device_id_type=MESH,
    )


def spread(count, me, device_of, src_of, dst, send_sem, recv_sem):
    pltpu.make_async_copy(src_of(me), dst, recv_sem).start()

    middle = count // 2

    def step(index, carry):
        offset = jnp.where(index < count - middle, middle + index, count - 1 - index)
        peer = lax.rem(me + offset, count)
        send_to(src_of(peer), dst, send_sem, recv_sem, device_of(peer)).start()
        return carry

    lax.fori_loop(0, count - 1, step, 0)


def greet(count, me, device_of):
    def step(offset, carry):
        peer = lax.rem(me + offset, count)
        pl.semaphore_signal(
            pltpu.get_barrier_semaphore(), inc=1, device_id=device_of(peer), device_id_type=MESH
        )
        return carry

    lax.fori_loop(1, count, step, 0)


def rows_of(index, count):
    return pl.ds(pl.multiple_of(index * count, count), count)


def grad_kernel(
    sizes,
    a_ref,
    w_ref,
    li_ref,
    query_ref,
    value_ref,
    out_ref,
    mid_ref,
    li_buf,
    dw_buf,
    t_buf,
    a_buf,
    w_buf,
    w_far,
    c_part,
    c_own,
    c_recv,
    x_send,
    x_recv,
    d_send,
    d_recv,
    mid_part,
    mid_recv,
    mid_sum,
    mid_all,
    t_sems,
    first_sems,
    w_sems,
    far_sems,
    twin_sems,
    ring_send,
    ring_recv,
    c_sems,
    c_arrived,
    x_sems,
    x_arrived,
    d_sems,
    m_sems,
    gate,
    in_sems,
):
    gx, gy, gz = sizes
    col, lev, place = lax.axis_index("gx"), lax.axis_index("gy"), lax.axis_index("gz")
    far, core = place // 2, lax.rem(place, 2)
    sides = gx // 2
    near_x, side = col // sides, lax.rem(col, sides)
    slots = gy * gz
    slot_me = lev * gz + place
    seq, width = a_ref.shape
    heads = w_ref.shape[0]
    unit = seq // slots
    chunk = unit * gz
    last = gy // 2

    def slot_device(index):
        return (col, index // gz, lax.rem(index, gz))

    def plane_device(index):
        return (index // gz, lev, lax.rem(index, gz))

    copies = [
        pltpu.make_async_copy(li_ref, li_buf, in_sems.at[0]),
        pltpu.make_async_copy(query_ref, dw_buf.at[0, :R], in_sems.at[1]),
        pltpu.make_async_copy(value_ref, dw_buf.at[0, R : 2 * R], in_sems.at[2]),
        pltpu.make_async_copy(query_ref, dw_buf.at[1, 2 * R : 3 * R], in_sems.at[3]),
        pltpu.make_async_copy(value_ref, dw_buf.at[1, 3 * R :], in_sems.at[4]),
    ]
    for copy in copies:
        copy.start()
    none = jnp.zeros((2 * R, width), jnp.bfloat16)
    dw_buf[0, 2 * R :] = none
    dw_buf[1, : 2 * R] = none

    greet(slots, slot_me, slot_device)
    greet(gx * gz, col * gz + place, plane_device)

    packed = seq // 2
    for copy in copies:
        copy.wait()
    lanes = (((1,), (1,)), ((), ()))
    mid_part[...] = lax.dot_general(
        li_buf[:packed, :], dw_buf[0], lanes, preferred_element_type=jnp.float32
    ) + lax.dot_general(li_buf[packed:, :], dw_buf[1], lanes, preferred_element_type=jnp.float32)

    pl.semaphore_wait(pltpu.get_barrier_semaphore(), slots - 1 + gx * gz - 1)

    def level_send(away):
        other = lax.rem(lev + away, gy)
        return send_to(
            a_ref.at[rows_of(other, chunk)],
            t_buf.at[lev],
            t_sems.at[0, away],
            t_sems.at[1, away],
            (col, other, place),
        )

    order = [1, gy - 1]
    for away in range(2, last):
        order += [away, gy - away]
    order.append(last)
    for away in order:
        level_send(away).start()

    def column_send(to, block):
        def one(index, carry):
            at = lax.rem(place + index, gz)
            source = block.at[rows_of(at, unit)]
            target = a_buf.at[place, 0, rows_of(side * 2 + near_x, unit)]
            mine = jnp.logical_and(col == to, at == place)

            @pl.when(mine)
            def _():
                pltpu.make_async_copy(source, target, first_sems.at[1]).start()

            @pl.when(jnp.logical_not(mine))
            def _():
                send_to(
                    source, target, first_sems.at[0], first_sems.at[1], (to, lev, at)
                ).start()

            return carry

        lax.fori_loop(0, gz, one, 0)

    column_send(lev, a_ref.at[rows_of(lev, chunk)])

    sibling = (col, lev, far * 2 + 1 - core)
    opposite = (col, lev, (1 - far) * 2 + core)
    shares = 4
    band = heads // shares
    own_w = pltpu.make_async_copy(w_ref, w_buf.at[0], w_sems.at[0])
    own_w.start()
    twin_w = send_to(w_ref, w_buf.at[1], w_sems.at[1], w_sems.at[2], sibling)
    twin_w.start()

    def far_w(share):
        return send_to(
            w_ref.at[pl.ds(share * band, band)],
            w_far.at[share, 0],
            far_sems.at[0, share],
            far_sems.at[1, share],
            opposite,
        )

    def pass_w(share):
        return send_to(
            w_far.at[share, 0],
            w_far.at[share, 1],
            twin_sems.at[0, share],
            twin_sems.at[1, share],
            sibling,
        )

    far_w(0).start()

    for away in order:
        other = lax.rem(lev + gy - away, gy)
        level_send(away).wait_recv()
        column_send(other, t_buf.at[other])

    up = (col, lax.rem(lev + 1, gy), place)
    down = (col, lax.rem(lev + gy - 1, gy), place)

    def ring(way, hop, which):
        parts = slice(2 * which, 2 * which + 2)
        start = 2 * hop - 3 + way if hop > 1 else 0
        end = 2 * hop - 1 + (way if hop < last else 0)
        index = 2 * (hop - 1) + (which if hop < last else 0)
        return send_to(
            a_buf.at[parts, start],
            a_buf.at[parts, end],
            ring_send.at[way, index],
            ring_recv.at[way, index],
            (up, down)[way],
        )

    cut = gy - 2

    def products(start, steps, weights):
        total = jnp.zeros((steps * gx * unit, weights(0).shape[0]), jnp.float32)
        for part in range(gz):
            total += lax.dot_general(
                a_buf[part, start : start + steps].reshape(steps * gx * unit, width),
                weights(part),
                (((1,), (1,)), ((), ())),
                preferred_element_type=jnp.float32,
            )
        return total

    def keep(block, start, steps, columns, total):
        total = total.reshape(steps, sides, 2, unit, total.shape[1])
        c_part[block, start : start + steps, :, :, :, columns] = total.astype(jnp.bfloat16)
        for way in range(sides):

            @pl.when(side == way)
            def _():
                c_own[block, start : start + steps, :, :, columns] = total[:, way]

    def give(blocks, start, steps, columns, kind):
        for at, end, group in (
            (start, min(start + steps, cut), kind),
            (max(start, cut), start + steps, 1),
        ):
            if end > at:
                for away in range(1, sides):
                    other = lax.rem(side + away, sides)
                    send_to(
                        c_part.at[blocks, at:end, other, :, :, columns],
                        c_recv.at[away - 1, blocks, at:end, :, :, columns],
                        c_sems.at[0],
                        c_arrived.at[group],
                        (near_x * sides + other, lev, place),
                    ).start()

    def near(start, steps):
        def one_block(block, carry):
            total = products(
                start, steps, lambda part: w_buf[block, :, part * width : (part + 1) * width]
            )
            keep(block, start, steps, slice(0, heads), total)
            give(pl.ds(block, 1), start, steps, slice(0, heads), 0)
            return carry

        lax.fori_loop(0, 2, one_block, 0)

    def far_part(start, share):
        total = products(
            start,
            2,
            lambda part: w_far[share, :, :, part * width : (part + 1) * width].reshape(
                2 * band, width
            ),
        )
        columns = slice(share * band, (share + 1) * band)
        for index in range(2):
            keep(2 + index, start, 2, columns, total[:, index * band : (index + 1) * band])
        give(slice(2, 4), start, 2, columns, 2)

    drain(a_buf.at[: gz - 1, 0], first_sems.at[0])
    drain(a_buf.at[gz - 1, 0, : (gx - 1) * unit], first_sems.at[0])

    def gate_signal(offset, carry):
        peer = lax.rem(near_x * gz + place + offset, 2 * gz)
        pl.semaphore_signal(
            gate,
            inc=1,
            device_id=(peer // gz * sides + side, lev, lax.rem(peer, gz)),
            device_id_type=MESH,
        )
        return carry

    lax.fori_loop(1, 2 * gz, gate_signal, 0)
    drain(a_buf.at[:, 0], first_sems.at[1])
    for which in range(2):
        for way in range(2):
            ring(way, 1, which).start()
    piece = packed // slots
    spread(
        slots,
        slot_me,
        slot_device,
        lambda index: mid_part.at[rows_of(index, piece)],
        mid_recv.at[slot_me],
        m_sems.at[0],
        m_sems.at[1],
    )

    pl.semaphore_wait(gate, 2 * gz - 1)
    far_w(1).start()
    own_w.wait()
    twin_w.wait_recv()
    near(0, 1)
    far_w(0).wait_recv()
    pass_w(0).start()
    for hop in range(1, last):
        for which in range(2):
            for way in range(2):
                ring(way, hop, which).wait_recv()
                if hop < last - 1 or way == which:
                    ring(way, hop + 1, which).start()
        near(2 * hop - 1, 2)
        if hop == 1:
            pass_w(0).wait_recv()
        for share in range(hop):
            far_part(2 * hop - 2, share)
        for share in [hop] if hop < last - 1 else range(hop, shares):
            far_w(share).wait_recv()
            pass_w(share).start()
            if share + 1 < shares:
                far_w(share).wait_send()
                far_w(share + 1).start()
            pass_w(share).wait_recv()
            for start in range(0, 2 * hop, 2):
                far_part(start, share)
        if hop == max(1, last - 2):
            drain(mid_recv, m_sems.at[1])
            mid_sum[...] = jnp.sum(mid_recv[...], axis=0)
            spread(
                slots,
                slot_me,
                slot_device,
                lambda index: mid_sum,
                mid_all.at[rows_of(slot_me, piece)],
                m_sems.at[2],
                m_sems.at[3],
            )
    ring(0, last, 0).wait_recv()
    ring(1, last, 1).wait_recv()
    near(gy - 1, 1)
    for share in range(shares):
        far_part(gy - 2, share)

    def hand_over(low, high, start, end, group):
        drain(c_recv.at[:, low:high, start:end], c_arrived.at[group])

        def one(block, carry):
            total = c_own[block, start:end]
            for away in range(sides - 1):
                total += c_recv[away, block, start:end].astype(jnp.float32)
            for half in range(2):

                @pl.when(near_x == half)
                def _():
                    x_send[block, start:end] = total[:, 1 - half].astype(jnp.bfloat16)
                    c_own[block, start:end, 0] = total[:, half]

            return carry

        lax.fori_loop(low, high, one, 0)
        send_to(
            x_send.at[low:high, start:end],
            x_recv.at[low:high, start:end],
            x_sems.at[group],
            x_arrived.at[group],
            ((1 - near_x) * sides + side, lev, place),
        ).start()

    def hand_out(low, high, start, end, group):
        drain(x_recv.at[low:high, start:end], x_arrived.at[group])

        def one(block, carry):
            total = c_own[block, start:end, 0] + x_recv[block, start:end].astype(jnp.float32)
            d_send[block, start:end] = total.astype(jnp.bfloat16)
            return carry

        lax.fori_loop(low, high, one, 0)
        for block in range(low, high):
            if block == 0:
                d_recv[place, start:end] = d_send[0, start:end]
                continue
            at = (far if block < 2 else 1 - far) * 2 + (1 - core if block % 2 else core)
            send_to(
                d_send.at[block, start:end],
                d_recv.at[place, start:end],
                d_sems.at[0],
                d_sems.at[1],
                (col, lev, at),
            ).start()

    hand_over(0, 2, 0, cut, 0)
    hand_over(2, 4, 0, cut, 2)
    hand_out(0, 2, 0, cut, 0)
    hand_over(0, 4, cut, gy, 1)
    hand_out(2, 4, 0, cut, 2)
    hand_out(0, 4, cut, gy, 1)

    for away in order:
        level_send(away).wait_send()
    twin_w.wait_send()
    far_w(0).wait_send()
    far_w(shares - 1).wait_send()
    for share in range(shares):
        pass_w(share).wait_send()
    for hop in range(1, last + 1):
        for which in range(2):
            for way in range(2):
                if hop < last or way == which:
                    ring(way, hop, which).wait_send()
    drain(mid_recv.at[: slots - 1], m_sems.at[0])
    drain(mid_recv.at[: slots - 1], m_sems.at[2])
    drain(mid_all, m_sems.at[3])
    mid_ref[...] = mid_all[...]
    drain(c_part.at[:, : gy * (sides - 1) // sides], c_sems.at[0])
    drain(x_send.at[:2, :cut], x_sems.at[0])
    drain(x_send.at[:, cut:], x_sems.at[1])
    drain(x_send.at[2:, :cut], x_sems.at[2])
    drain(d_send.at[1:], d_sems.at[0])
    drain(d_send.at[1:], d_sems.at[1])

    for start in range(gy):
        hop = (start + 1) // 2
        level = lax.rem(lev + (gy - hop if start % 2 else hop), gy)

        def one_place(at, carry):
            out_ref[rows_of(level * gz + at, unit), :] = d_recv[at, start]
            return carry

        lax.fori_loop(0, gz, one_place, 0)


def grad_call(sizes, out_grad, out_weight, layer_input, query_down, value_down):
    gx, gy, gz = sizes
    seq, width = out_grad.shape
    heads, depth = out_weight.shape
    slots = gy * gz
    unit = seq // slots
    piece = seq // 2 // slots
    sides = gx // 2
    vmem = pl.BlockSpec(memory_space=pltpu.VMEM)
    anywhere = pl.BlockSpec(memory_space=pl.ANY)
    low = jnp.bfloat16
    return pl.pallas_call(
        functools.partial(grad_kernel, sizes),
        out_shape=(
            jax.ShapeDtypeStruct((seq, heads), low),
            jax.ShapeDtypeStruct((seq // 2, 128), jnp.float32),
        ),
        in_specs=[anywhere] * 5,
        out_specs=(vmem, vmem),
        scratch_shapes=[
            pltpu.VMEM((seq, width), low),
            pltpu.VMEM((2, 4 * R, width), low),
            pltpu.VMEM((gy, unit * gz, width), low),
            pltpu.VMEM((gz, gy, gx * unit, width), low),
            pltpu.VMEM((2, heads, depth), low),
            pltpu.VMEM((4, 2, heads // 4, depth), low),
            pltpu.VMEM((gz, gy, sides, 2, unit, heads), low),
            pltpu.VMEM((gz, gy, 2, unit, heads), jnp.float32),
            pltpu.VMEM((sides - 1, gz, gy, 2, unit, heads), low),
            pltpu.VMEM((gz, gy, unit, heads), low),
            pltpu.VMEM((gz, gy, unit, heads), low),
            pltpu.VMEM((gz, gy, unit, heads), low),
            pltpu.VMEM((gz, gy, unit, heads), low),
            pltpu.VMEM((seq // 2, 128), jnp.float32),
            pltpu.VMEM((slots, piece, 128), jnp.float32),
            pltpu.VMEM((piece, 128), jnp.float32),
            pltpu.VMEM((seq // 2, 128), jnp.float32),
            pltpu.SemaphoreType.DMA((2, gy)),
            pltpu.SemaphoreType.DMA((2,)),
            pltpu.SemaphoreType.DMA((3,)),
            pltpu.SemaphoreType.DMA((2, 4)),
            pltpu.SemaphoreType.DMA((2, 4)),
            pltpu.SemaphoreType.DMA((2, gy - 1)),
            pltpu.SemaphoreType.DMA((2, gy - 1)),
            pltpu.SemaphoreType.DMA((1,)),
            pltpu.SemaphoreType.DMA((3,)),
            pltpu.SemaphoreType.DMA((3,)),
            pltpu.SemaphoreType.DMA((3,)),
            pltpu.SemaphoreType.DMA((2,)),
            pltpu.SemaphoreType.DMA((4,)),
            pltpu.SemaphoreType.REGULAR,
            pltpu.SemaphoreType.DMA((5,)),
        ],
        compiler_params=pltpu.CompilerParams(
            collective_id=0, has_side_effects=True, vmem_limit_bytes=60 << 20
        ),
        cost_estimate=pl.CostEstimate(
            flops=2 * seq * heads * depth * gx, bytes_accessed=16 << 20, transcendentals=0
        ),
    )(out_grad, out_weight, layer_input, query_down.T, value_down.T)


def split_low(array):
    high = array.astype(jnp.bfloat16)
    return high, (array - high.astype(jnp.float32)).astype(jnp.bfloat16)


def product(left, right, left_dim, right_dim):
    return lax.dot_general(
        left, right, (((left_dim,), (right_dim,)), ((), ())), preferred_element_type=jnp.float32
    )


def sum_kernel(
    sizes,
    lengths_ref,
    grad_ref,
    mid_ref,
    queries_ref,
    keys_any,
    values_any,
    up_any,
    value_up_any,
    li_ref,
    query_down_ref,
    raise_out,
    value_down_ref,
    value_out,
    keys_ref,
    values_ref,
    up_ref,
    value_up_ref,
    query_grad,
    value_grad,
    factor_ref,
    raise_ref,
    value_ref,
    factor_recv,
    factor_sum,
    factor_all,
    raise_recv,
    raise_sum,
    raise_all,
    value_recv,
    value_sum,
    value_plane,
    value_done,
    value_level,
    value_all,
    down_part,
    down_recv,
    down_sum,
    down_all,
    sends,
    recvs,
    in_sems,
):
    gx, gy, gz = sizes
    col, lev, place = lax.axis_index("gx"), lax.axis_index("gy"), lax.axis_index("gz")
    slots = gy * gz
    slot_me = lev * gz + place
    seq, width = queries_ref.shape
    head_count = width // HD
    kv = slot_me * head_count // (HQ // KVH)
    kv_columns = pl.ds(pl.multiple_of(kv * HD, HD), HD)

    def slot_device(index):
        return (col, index // gz, lax.rem(index, gz))

    def column_device(index):
        return (index, lev, place)

    def level_device(index):
        return (col, index, place)

    def place_device(index):
        return (col, lev, index)

    copies = [
        pltpu.make_async_copy(keys_any.at[:, kv_columns], keys_ref, in_sems.at[0]),
        pltpu.make_async_copy(values_any.at[:, kv_columns], values_ref, in_sems.at[1]),
        pltpu.make_async_copy(up_any, up_ref.at[0, :R], in_sems.at[2]),
        pltpu.make_async_copy(up_any, up_ref.at[1, 2 * R : 3 * R], in_sems.at[3]),
        pltpu.make_async_copy(
            value_up_any.at[:, kv_columns], value_up_ref.at[0, R : 2 * R], in_sems.at[4]
        ),
        pltpu.make_async_copy(
            value_up_any.at[:, kv_columns], value_up_ref.at[1, 3 * R :], in_sems.at[5]
        ),
    ]
    for copy in copies:
        copy.start()
    up_ref[0, R:] = jnp.zeros((3 * R, width), jnp.bfloat16)
    up_ref[1, : 2 * R] = jnp.zeros((2 * R, width), jnp.bfloat16)
    up_ref[1, 3 * R :] = jnp.zeros((R, width), jnp.bfloat16)
    value_up_ref[0, :R] = jnp.zeros((R, HD), jnp.bfloat16)
    value_up_ref[0, 2 * R :] = jnp.zeros((2 * R, HD), jnp.bfloat16)
    value_up_ref[1, : 3 * R] = jnp.zeros((3 * R, HD), jnp.bfloat16)

    greet(slots, slot_me, slot_device)
    greet(gx, col, column_device)

    for copy in copies:
        copy.wait()
    length = lengths_ref[0]
    score_scale = HD ** (-0.5)
    value_grad[...] = jnp.zeros_like(value_grad)
    packed = seq // 2

    def one_head(head, carry):
        columns = pl.ds(pl.multiple_of(head * HD, HD), HD)
        for block in range(2):
            rows = slice(block * packed, (block + 1) * packed)
            span = (block + 1) * packed
            keys, values = keys_ref[:span], values_ref[:span]
            shape = (packed, span)
            row = lax.broadcasted_iota(jnp.int32, shape, 0) + block * packed
            key = lax.broadcasted_iota(jnp.int32, shape, 1)
            scores = product(queries_ref[rows, columns], keys, 1, 1) * score_scale
            scores = jnp.where((key <= row) & (key < length), scores, mask_fill)
            raised = jnp.exp(scores - jnp.max(scores, axis=1, keepdims=True))
            attention = raised / jnp.sum(raised, axis=1, keepdims=True)
            grads = grad_ref[rows, columns]
            line = lax.broadcasted_iota(jnp.int32, grads.shape, 0) + block * packed
            grads = jnp.where(line < length, grads.astype(jnp.float32), 0.0).astype(jnp.bfloat16)
            value_grad[:span] += product(attention.astype(jnp.bfloat16), grads, 0, 0)
            prob_grad = product(grads, values, 1, 1)
            centre = jnp.sum(attention * prob_grad, axis=1, keepdims=True)
            score_grad = (attention * (prob_grad - centre)).astype(jnp.bfloat16)
            query_grad[rows, columns] = product(score_grad, keys, 1, 0) * score_scale
        return carry

    lax.fori_loop(0, head_count, one_head, 0)

    total = jnp.zeros((packed, 128), jnp.float32)
    raised = jnp.zeros((R, width), jnp.float32)
    value_part = jnp.zeros((R, HD), jnp.float32)
    mid_high, mid_low = split_low(mid_ref[...])
    for block in range(2):
        rows = slice(block * packed, (block + 1) * packed)
        high, low = split_low(query_grad[rows])
        total += product(high, up_ref[block], 1, 1) + product(low, up_ref[block], 1, 1)
        every = product(mid_high, high, 0, 0) + product(mid_low, high, 0, 0)
        every += product(mid_high, low, 0, 0)
        raised += every[block * 2 * R : block * 2 * R + R]
        high, low = split_low(value_grad[rows])
        total += product(high, value_up_ref[block], 1, 1)
        total += product(low, value_up_ref[block], 1, 1)
        every = product(mid_high, high, 0, 0) + product(mid_low, high, 0, 0)
        every += product(mid_high, low, 0, 0)
        value_part += every[block * 2 * R + R : (block + 1) * 2 * R]
    factor_ref[...] = total.reshape(factor_ref.shape)
    raised = adapter_scale * raised
    value_part = adapter_scale * value_part
    raise_ref[...] = jnp.concatenate(
        [raised[:, at : at + 128] for at in range(0, width, 128)], axis=0
    ).reshape(raise_ref.shape)
    per = R // gx
    value_ref[...] = jnp.zeros_like(value_ref)
    for at in range(gx):
        value_ref[at, :per] = value_part[at * per : (at + 1) * per]

    pl.semaphore_wait(pltpu.get_barrier_semaphore(), slots + gx - 2)

    spread(slots, slot_me, slot_device, lambda i: factor_ref.at[i], factor_recv.at[slot_me], sends.at[0], recvs.at[0])
    spread(gx, col, column_device, lambda i: value_ref.at[i], value_recv.at[col], sends.at[1], recvs.at[1])
    spread(gx, col, column_device, lambda i: raise_ref.at[i], raise_recv.at[col], sends.at[2], recvs.at[2])

    drain(factor_recv, recvs.at[0])
    factor_sum[...] = jnp.sum(factor_recv[...], axis=0)
    spread(slots, slot_me, slot_device, lambda i: factor_sum, factor_all.at[slot_me], sends.at[3], recvs.at[3])
    drain(value_recv, recvs.at[1])
    value_sum[...] = jnp.sum(value_recv[...], axis=0)
    spread(gz, place, place_device, lambda i: value_sum, value_plane.at[place], sends.at[4], recvs.at[4])
    drain(raise_recv, recvs.at[2])
    raise_sum[...] = jnp.sum(raise_recv[...], axis=0)
    spread(gx, col, column_device, lambda i: raise_sum, raise_all.at[col], sends.at[5], recvs.at[5])

    drain(factor_all, recvs.at[3])
    factor = factor_all[...].reshape(packed, 128)
    factor_high, factor_low = split_low(factor)

    def project(rows):
        block = li_ref[rows, :]
        dims = (((0,), (0,)), ((), ()))
        return lax.dot_general(
            block, factor_high, dims, preferred_element_type=jnp.float32
        ) + lax.dot_general(block, factor_low, dims, preferred_element_type=jnp.float32)

    first = project(slice(0, packed))
    second = project(slice(packed, 2 * packed))
    lane = lax.broadcasted_iota(jnp.int32, first.shape, 1)
    both = adapter_scale * jnp.where(lane < 64, first, second)
    both = both + pltpu.roll(both, 64, 1)
    rows = both.shape[0] // 2
    both = jnp.where(lane[:rows] < 64, both[:rows], both[rows:])
    down_part[...] = both.reshape(down_part.shape)
    spread(gx, col, column_device, lambda i: down_part.at[i], down_recv.at[col], sends.at[6], recvs.at[6])

    drain(value_plane, recvs.at[4])
    value_done[...] = jnp.sum(value_plane[...], axis=0)
    spread(gy, lev, level_device, lambda i: value_done, value_level.at[lev], sends.at[7], recvs.at[7])
    drain(value_level, recvs.at[7])
    spread(gx, col, column_device, lambda i: value_level, value_all.at[col], sends.at[8], recvs.at[8])

    drain(down_recv, recvs.at[6])
    down_sum[...] = jnp.sum(down_recv[...], axis=0)
    spread(gx, col, column_device, lambda i: down_sum, down_all.at[col], sends.at[9], recvs.at[9])

    drain(raise_all, recvs.at[5])
    raised = raise_all[...].reshape(-1, 128)
    for at in range(raised.shape[0] // R):
        raise_out[:, at * 128 : (at + 1) * 128] = raised[at * R : (at + 1) * R]
    drain(value_all, recvs.at[8])
    for at in range(gx):
        for level in range(gy):
            value_out[at * per : (at + 1) * per, level * 128 : (level + 1) * 128] = value_all[
                at, level, :per
            ]
    drain(down_all, recvs.at[9])
    turned = down_all[...].reshape(-1, 128).T
    query_down_ref[:, :rows] = turned[:R]
    query_down_ref[:, rows:] = turned[2 * R : 3 * R]
    value_down_ref[:, :rows] = turned[R : 2 * R]
    value_down_ref[:, rows:] = turned[3 * R :]
    drain(factor_recv.at[: slots - 1], sends.at[0])
    drain(value_recv.at[: gx - 1], sends.at[1])
    drain(raise_recv.at[: gx - 1], sends.at[2])
    drain(factor_all.at[: slots - 1], sends.at[3])
    drain(value_plane.at[: gz - 1], sends.at[4])
    drain(raise_all.at[: gx - 1], sends.at[5])
    drain(down_recv.at[: gx - 1], sends.at[6])
    drain(value_level.at[: gy - 1], sends.at[7])
    drain(value_all.at[: gx - 1], sends.at[8])
    drain(down_all.at[: gx - 1], sends.at[9])


def sum_call(
    sizes,
    attn_grad,
    middle,
    saved_queries,
    saved_keys,
    saved_values,
    query_up,
    value_up,
    layer_input,
    lengths,
):
    gx, gy, gz = sizes
    slots = gy * gz
    seq, width = layer_input.shape
    heads = saved_queries.shape[1]
    vmem = pl.BlockSpec(memory_space=pltpu.VMEM)
    anywhere = pl.BlockSpec(memory_space=pl.ANY)
    single, low = jnp.float32, jnp.bfloat16
    factor = (slots, seq // 2 // slots, 128)
    raised = (gx, R * heads // 128 // gx, 128)
    value = (gx, max(ROWS, R // gx), 128)
    down = (gx, width // gx // 2, 128)
    shapes = [
        ((seq, HD), low),
        ((seq, HD), low),
        ((2, 4 * R, heads), low),
        ((2, 4 * R, HD), low),
        ((seq, heads), single),
        ((seq, HD), single),
        (factor, single),
        (raised, single),
        (value, single),
        (factor, single),
        (factor[1:], single),
        (factor, single),
        (raised, single),
        (raised[1:], single),
        (raised, single),
        (value, single),
        (value[1:], single),
        ((gz,) + value[1:], single),
        (value[1:], single),
        ((gy,) + value[1:], single),
        ((gx, gy) + value[1:], single),
        (down, single),
        (down, single),
        (down[1:], single),
        (down, single),
    ]
    return pl.pallas_call(
        functools.partial(sum_kernel, sizes),
        out_shape=(
            jax.ShapeDtypeStruct((R, width), single),
            jax.ShapeDtypeStruct((R, heads), single),
            jax.ShapeDtypeStruct((R, width), single),
            jax.ShapeDtypeStruct((R, gy * 128), single),
        ),
        in_specs=[pl.BlockSpec(memory_space=pltpu.SMEM), vmem, vmem, vmem]
        + [anywhere] * 4
        + [vmem],
        out_specs=(vmem,) * 4,
        scratch_shapes=[pltpu.VMEM(shape, kind) for shape, kind in shapes]
        + [
            pltpu.SemaphoreType.DMA((10,)),
            pltpu.SemaphoreType.DMA((10,)),
            pltpu.SemaphoreType.DMA((6,)),
        ],
        compiler_params=pltpu.CompilerParams(
            collective_id=1, has_side_effects=True, vmem_limit_bytes=40 << 20
        ),
    )(
        lengths,
        attn_grad,
        middle,
        saved_queries,
        saved_keys,
        saved_values,
        query_up,
        value_up,
        layer_input,
    )


def body(
    sizes,
    out_grad,
    layer_input,
    out_weight,
    saved_queries,
    saved_keys,
    saved_values,
    query_down,
    query_up,
    value_down,
    value_up,
    lengths,
):
    attn_grad, middle = grad_call(
        sizes, out_grad, out_weight, layer_input, query_down, value_down
    )
    query_down_grad, query_up_grad, value_down_grad, value_up_grad = sum_call(
        sizes,
        attn_grad,
        middle,
        saved_queries,
        saved_keys,
        saved_values,
        query_up,
        value_up,
        layer_input,
        lengths,
    )
    return (query_down_grad.T, query_up_grad, value_down_grad.T, value_up_grad)


def solution(mesh):
    sizes = tuple(mesh.shape[name] for name in ("gx", "gy", "gz"))
    return jax.shard_map(
        functools.partial(body, sizes),
        mesh=mesh,
        in_specs=(
            P("gx", ("gy", "gz")),
            P("gx", ("gy", "gz")),
            P(("gy", "gz"), "gx"),
            P("gx", ("gy", "gz")),
            P("gx", None),
            P("gx", None),
            P(("gy", "gz"), None),
            P(None, ("gy", "gz")),
            P(("gy", "gz"), None),
            P(),
            P("gx"),
        ),
        out_specs=(P(("gy", "gz"), None), P(None, ("gy", "gz")), P(("gy", "gz"), None), P()),
        check_vma=False,
    )
```

```python
import functools

import jax
import jax.numpy as jnp
from jax import lax
from jax.experimental import pallas as pl
from jax.experimental.pallas import tpu as pltpu
from jax.sharding import PartitionSpec as P

HQ = 128
KVH = 8
HD = 128
R = 32

adapter_scale = 2.0
mask_fill = -1e30
MESH = pl.DeviceIdType.MESH
ROWS = 8


def drain(ref, sem):
    pltpu.make_async_copy(ref, ref, sem).wait()


def send_to(src, dst, send_sem, recv_sem, device):
    return pltpu.make_async_remote_copy(
        src_ref=src,
        dst_ref=dst,
        send_sem=send_sem,
        recv_sem=recv_sem,
        device_id=device,
        device_id_type=MESH,
    )


def spread(count, me, device_of, src_of, dst, send_sem, recv_sem):
    pltpu.make_async_copy(src_of(me), dst, recv_sem).start()

    middle = count // 2

    def step(index, carry):
        offset = jnp.where(index < count - middle, middle + index, count - 1 - index)
        peer = lax.rem(me + offset, count)
        send_to(src_of(peer), dst, send_sem, recv_sem, device_of(peer)).start()
        return carry

    lax.fori_loop(0, count - 1, step, 0)


def greet(count, me, device_of):
    def step(offset, carry):
        peer = lax.rem(me + offset, count)
        pl.semaphore_signal(
            pltpu.get_barrier_semaphore(), inc=1, device_id=device_of(peer), device_id_type=MESH
        )
        return carry

    lax.fori_loop(1, count, step, 0)


def rows_of(index, count):
    return pl.ds(pl.multiple_of(index * count, count), count)


def grad_kernel(
    sizes,
    a_ref,
    w_ref,
    li_ref,
    query_ref,
    value_ref,
    out_ref,
    mid_ref,
    li_buf,
    dw_buf,
    t_buf,
    a_buf,
    w_buf,
    w_far,
    c_part,
    c_own,
    c_recv,
    x_send,
    x_recv,
    d_send,
    d_recv,
    mid_part,
    mid_recv,
    mid_sum,
    mid_all,
    t_sems,
    first_sems,
    w_sems,
    far_sems,
    twin_sems,
    ring_send,
    ring_recv,
    c_sems,
    c_arrived,
    x_sems,
    x_arrived,
    d_sems,
    m_sems,
    gate,
    in_sems,
    attend,
):
    gx, gy, gz = sizes
    col, lev, place = lax.axis_index("gx"), lax.axis_index("gy"), lax.axis_index("gz")
    far, core = place // 2, lax.rem(place, 2)
    sides = gx // 2
    near_x, side = col // sides, lax.rem(col, sides)
    slots = gy * gz
    slot_me = lev * gz + place
    seq, width = a_ref.shape
    heads = w_ref.shape[0]
    unit = seq // slots
    chunk = unit * gz
    last = gy // 2

    def slot_device(index):
        return (col, index // gz, lax.rem(index, gz))

    def plane_device(index):
        return (index // gz, lev, lax.rem(index, gz))

    copies = [
        pltpu.make_async_copy(li_ref, li_buf, in_sems.at[0]),
        pltpu.make_async_copy(query_ref, dw_buf.at[0, :R], in_sems.at[1]),
        pltpu.make_async_copy(value_ref, dw_buf.at[0, R : 2 * R], in_sems.at[2]),
        pltpu.make_async_copy(query_ref, dw_buf.at[1, 2 * R : 3 * R], in_sems.at[3]),
        pltpu.make_async_copy(value_ref, dw_buf.at[1, 3 * R :], in_sems.at[4]),
    ]
    for copy in copies:
        copy.start()
    none = jnp.zeros((2 * R, width), jnp.bfloat16)
    dw_buf[0, 2 * R :] = none
    dw_buf[1, : 2 * R] = none

    greet(slots, slot_me, slot_device)
    greet(gx * gz, col * gz + place, plane_device)

    packed = seq // 2
    for copy in copies:
        copy.wait()
    lanes = (((1,), (1,)), ((), ()))
    mid_part[...] = lax.dot_general(
        li_buf[:packed, :], dw_buf[0], lanes, preferred_element_type=jnp.float32
    ) + lax.dot_general(li_buf[packed:, :], dw_buf[1], lanes, preferred_element_type=jnp.float32)

    pl.semaphore_wait(pltpu.get_barrier_semaphore(), slots - 1 + gx * gz - 1)

    def level_send(away):
        other = lax.rem(lev + away, gy)
        return send_to(
            a_ref.at[rows_of(other, chunk)],
            t_buf.at[lev],
            t_sems.at[0, away],
            t_sems.at[1, away],
            (col, other, place),
        )

    order = [last]
    for away in range(last - 1, 0, -1):
        order += [away, gy - away]
    for away in order:
        level_send(away).start()

    def column_send(to, block):
        def one(index, carry):
            at = lax.rem(place + index, gz)
            source = block.at[rows_of(at, unit)]
            target = a_buf.at[place, 0, rows_of(side * 2 + near_x, unit)]
            mine = jnp.logical_and(col == to, at == place)

            @pl.when(mine)
            def _():
                pltpu.make_async_copy(source, target, first_sems.at[1]).start()

            @pl.when(jnp.logical_not(mine))
            def _():
                send_to(
                    source, target, first_sems.at[0], first_sems.at[1], (to, lev, at)
                ).start()

            return carry

        lax.fori_loop(0, gz, one, 0)

    column_send(lev, a_ref.at[rows_of(lev, chunk)])

    sibling = (col, lev, far * 2 + 1 - core)
    opposite = (col, lev, (1 - far) * 2 + core)
    shares = 4
    band = heads // shares
    own_w = pltpu.make_async_copy(w_ref, w_buf.at[0], w_sems.at[0])
    own_w.start()
    twin_w = send_to(w_ref, w_buf.at[1], w_sems.at[1], w_sems.at[2], sibling)
    twin_w.start()

    def far_w(share):
        return send_to(
            w_ref.at[pl.ds(share * band, band)],
            w_far.at[share, 0],
            far_sems.at[0, share],
            far_sems.at[1, share],
            opposite,
        )

    def pass_w(share):
        return send_to(
            w_far.at[share, 0],
            w_far.at[share, 1],
            twin_sems.at[0, share],
            twin_sems.at[1, share],
            sibling,
        )

    far_w(0).start()

    for away in order:
        other = lax.rem(lev + gy - away, gy)
        level_send(away).wait_recv()
        column_send(other, t_buf.at[other])

    up = (col, lax.rem(lev + 1, gy), place)
    down = (col, lax.rem(lev + gy - 1, gy), place)

    def ring(way, hop, which):
        parts = slice(2 * which, 2 * which + 2)
        start = 2 * hop - 3 + way if hop > 1 else 0
        end = 2 * hop - 1 + (way if hop < last else 0)
        index = 2 * (hop - 1) + (which if hop < last else 0)
        return send_to(
            a_buf.at[parts, start],
            a_buf.at[parts, end],
            ring_send.at[way, index],
            ring_recv.at[way, index],
            (up, down)[way],
        )

    cut = gy - 2

    def products(start, steps, weights):
        total = jnp.zeros((steps * gx * unit, weights(0).shape[0]), jnp.float32)
        for part in range(gz):
            total += lax.dot_general(
                a_buf[part, start : start + steps].reshape(steps * gx * unit, width),
                weights(part),
                (((1,), (1,)), ((), ())),
                preferred_element_type=jnp.float32,
            )
        return total

    def keep(block, start, steps, columns, total):
        total = total.reshape(steps, sides, 2, unit, total.shape[1])
        c_part[block, start : start + steps, :, :, :, columns] = total.astype(jnp.bfloat16)
        for way in range(sides):

            @pl.when(side == way)
            def _():
                c_own[block, start : start + steps, :, :, columns] = total[:, way]

    def give(blocks, start, steps, columns, kind):
        for at, end, group in (
            (start, min(start + steps, cut), kind),
            (max(start, cut), start + steps, 1),
        ):
            if end > at:
                for away in range(1, sides):
                    other = lax.rem(side + away, sides)
                    send_to(
                        c_part.at[blocks, at:end, other, :, :, columns],
                        c_recv.at[away - 1, blocks, at:end, :, :, columns],
                        c_sems.at[0],
                        c_arrived.at[group],
                        (near_x * sides + other, lev, place),
                    ).start()

    def near(start, steps):
        def one_block(block, carry):
            total = products(
                start, steps, lambda part: w_buf[block, :, part * width : (part + 1) * width]
            )
            keep(block, start, steps, slice(0, heads), total)
            give(pl.ds(block, 1), start, steps, slice(0, heads), 0)
            return carry

        lax.fori_loop(0, 2, one_block, 0)

    def far_part(start, share):
        total = products(
            start,
            2,
            lambda part: w_far[share, :, :, part * width : (part + 1) * width].reshape(
                2 * band, width
            ),
        )
        columns = slice(share * band, (share + 1) * band)
        for index in range(2):
            keep(2 + index, start, 2, columns, total[:, index * band : (index + 1) * band])
        give(slice(2, 4), start, 2, columns, 2)

    attend(0)
    drain(a_buf.at[: gz - 1, 0], first_sems.at[0])
    drain(a_buf.at[gz - 1, 0, : (gx - 1) * unit], first_sems.at[0])

    def gate_signal(offset, carry):
        peer = lax.rem(near_x * gz + place + offset, 2 * gz)
        pl.semaphore_signal(
            gate,
            inc=1,
            device_id=(peer // gz * sides + side, lev, lax.rem(peer, gz)),
            device_id_type=MESH,
        )
        return carry

    lax.fori_loop(1, 2 * gz, gate_signal, 0)
    drain(a_buf.at[:, 0], first_sems.at[1])
    for which in range(2):
        for way in range(2):
            ring(way, 1, which).start()
    piece = packed // slots
    spread(
        slots,
        slot_me,
        slot_device,
        lambda index: mid_part.at[rows_of(index, piece)],
        mid_recv.at[slot_me],
        m_sems.at[0],
        m_sems.at[1],
    )

    pl.semaphore_wait(gate, 2 * gz - 1)
    far_w(1).start()
    own_w.wait()
    twin_w.wait_recv()
    near(0, 1)
    attend(1)
    far_w(0).wait_recv()
    pass_w(0).start()
    for hop in range(1, last):
        for which in range(2):
            for way in range(2):
                ring(way, hop, which).wait_recv()
                if hop < last - 1 or way == which:
                    ring(way, hop + 1, which).start()
        near(2 * hop - 1, 2)
        if hop < last - 1:
            attend(hop + 1)
        if hop == 1:
            pass_w(0).wait_recv()
        for share in range(hop):
            far_part(2 * hop - 2, share)
        for share in [hop] if hop < last - 1 else range(hop, shares):
            far_w(share).wait_recv()
            pass_w(share).start()
            if share + 1 < shares:
                far_w(share).wait_send()
                far_w(share + 1).start()
            pass_w(share).wait_recv()
            for start in range(0, 2 * hop, 2):
                far_part(start, share)
        if hop == max(1, last - 2):
            drain(mid_recv, m_sems.at[1])
            mid_sum[...] = jnp.sum(mid_recv[...], axis=0)
            spread(
                slots,
                slot_me,
                slot_device,
                lambda index: mid_sum,
                mid_all.at[rows_of(slot_me, piece)],
                m_sems.at[2],
                m_sems.at[3],
            )
    ring(0, last, 0).wait_recv()
    ring(1, last, 1).wait_recv()
    near(gy - 1, 1)
    for share in range(shares):
        far_part(gy - 2, share)

    def hand_over(low, high, start, end, group):
        drain(c_recv.at[:, low:high, start:end], c_arrived.at[group])

        def one(block, carry):
            total = c_own[block, start:end]
            for away in range(sides - 1):
                total += c_recv[away, block, start:end].astype(jnp.float32)
            for half in range(2):

                @pl.when(near_x == half)
                def _():
                    x_send[block, start:end] = total[:, 1 - half].astype(jnp.bfloat16)
                    c_own[block, start:end, 0] = total[:, half]

            return carry

        lax.fori_loop(low, high, one, 0)
        send_to(
            x_send.at[low:high, start:end],
            x_recv.at[low:high, start:end],
            x_sems.at[group],
            x_arrived.at[group],
            ((1 - near_x) * sides + side, lev, place),
        ).start()

    def hand_out(low, high, start, end, group):
        drain(x_recv.at[low:high, start:end], x_arrived.at[group])

        def one(block, carry):
            total = c_own[block, start:end, 0] + x_recv[block, start:end].astype(jnp.float32)
            d_send[block, start:end] = total.astype(jnp.bfloat16)
            return carry

        lax.fori_loop(low, high, one, 0)
        for block in range(low, high):
            if block == 0:
                d_recv[place, start:end] = d_send[0, start:end]
                continue
            at = (far if block < 2 else 1 - far) * 2 + (1 - core if block % 2 else core)
            send_to(
                d_send.at[block, start:end],
                d_recv.at[place, start:end],
                d_sems.at[0],
                d_sems.at[1],
                (col, lev, at),
            ).start()

    hand_over(0, 2, 0, cut, 0)
    hand_over(2, 4, 0, cut, 2)
    hand_out(0, 2, 0, cut, 0)
    hand_over(0, 4, cut, gy, 1)
    hand_out(2, 4, 0, cut, 2)
    hand_out(0, 4, cut, gy, 1)

    for away in order:
        level_send(away).wait_send()
    twin_w.wait_send()
    far_w(0).wait_send()
    far_w(shares - 1).wait_send()
    for share in range(shares):
        pass_w(share).wait_send()
    for hop in range(1, last + 1):
        for which in range(2):
            for way in range(2):
                if hop < last or way == which:
                    ring(way, hop, which).wait_send()
    drain(mid_recv.at[: slots - 1], m_sems.at[0])
    drain(mid_recv.at[: slots - 1], m_sems.at[2])
    drain(mid_all, m_sems.at[3])
    mid_ref[...] = mid_all[...]
    drain(c_part.at[:, : gy * (sides - 1) // sides], c_sems.at[0])
    drain(x_send.at[:2, :cut], x_sems.at[0])
    drain(x_send.at[:, cut:], x_sems.at[1])
    drain(x_send.at[2:, :cut], x_sems.at[2])
    drain(d_send.at[1:], d_sems.at[0])
    drain(d_send.at[1:], d_sems.at[1])

    for start in range(gy):
        hop = (start + 1) // 2
        level = lax.rem(lev + (gy - hop if start % 2 else hop), gy)

        def one_place(at, carry):
            out_ref[rows_of(level * gz + at, unit), :] = d_recv[at, start]
            return carry

        lax.fori_loop(0, gz, one_place, 0)


def split_low(array):
    high = array.astype(jnp.bfloat16)
    return high, (array - high.astype(jnp.float32)).astype(jnp.bfloat16)


def product(left, right, left_dim, right_dim):
    return lax.dot_general(
        left, right, (((left_dim,), (right_dim,)), ((), ())), preferred_element_type=jnp.float32
    )


def attention_kernel(
    lengths_ref,
    queries_ref,
    keys_ref,
    attention_ref,
    head,
):
    seq = queries_ref.shape[0]
    packed = seq // 2
    length = lengths_ref[0]
    columns = pl.ds(pl.multiple_of(head * HD, HD), HD)
    for block in range(2):
        rows = slice(block * packed, (block + 1) * packed)
        span = (block + 1) * packed
        shape = (packed, span)
        row = lax.broadcasted_iota(jnp.int32, shape, 0) + block * packed
        key = lax.broadcasted_iota(jnp.int32, shape, 1)
        scores = product(queries_ref[rows, columns], keys_ref[:span], 1, 1) * HD ** (-0.5)
        scores = jnp.where((key <= row) & (key < length), scores, mask_fill)
        raised = jnp.exp(scores - jnp.max(scores, axis=1, keepdims=True))
        attention_ref[head, rows, :span] = raised / jnp.sum(raised, axis=1, keepdims=True)


def sum_kernel(
    sizes,
    lengths_ref,
    out_ref,
    li_ref,
    grad_ref,
    mid_ref,
    keys_ref,
    values_ref,
    up_ref,
    value_up_ref,
    attention_ref,
    query_grad,
    value_grad,
    factor_ref,
    raise_ref,
    value_ref,
    factor_recv,
    factor_sum,
    factor_all,
    raise_recv,
    raise_sum,
    raise_all,
    value_recv,
    value_sum,
    value_plane,
    value_done,
    value_level,
    value_all,
    down_part,
    down_recv,
    down_sum,
    down_all,
    sends,
    recvs,
):
    gx, gy, gz = sizes
    col, lev, place = lax.axis_index("gx"), lax.axis_index("gy"), lax.axis_index("gz")
    slots = gy * gz
    slot_me = lev * gz + place
    seq, width = query_grad.shape
    packed = seq // 2
    length = lengths_ref[0]

    def slot_device(index):
        return (col, index // gz, lax.rem(index, gz))

    def column_device(index):
        return (index, lev, place)

    def level_device(index):
        return (col, index, place)

    def place_device(index):
        return (col, lev, index)

    value_grad[...] = jnp.zeros_like(value_grad)

    def one_head(head, carry):
        columns = pl.ds(pl.multiple_of(head * HD, HD), HD)
        for block in range(2):
            rows = slice(block * packed, (block + 1) * packed)
            span = (block + 1) * packed
            attention = attention_ref[head, rows, :span]
            grads = grad_ref[rows, columns]
            line = lax.broadcasted_iota(jnp.int32, grads.shape, 0) + block * packed
            grads = jnp.where(line < length, grads.astype(jnp.float32), 0.0).astype(jnp.bfloat16)
            value_grad[:span] += product(attention.astype(jnp.bfloat16), grads, 0, 0)
            prob_grad = product(grads, values_ref[:span], 1, 1)
            centre = jnp.sum(attention * prob_grad, axis=1, keepdims=True)
            score_grad = (attention * (prob_grad - centre)).astype(jnp.bfloat16)
            query_grad[rows, columns] = product(score_grad, keys_ref[:span], 1, 0) * HD ** (-0.5)
        return carry

    lax.fori_loop(0, width // HD, one_head, 0)

    total = jnp.zeros((packed, 128), jnp.float32)
    raised = jnp.zeros((R, width), jnp.float32)
    value_part = jnp.zeros((R, HD), jnp.float32)
    mid_high, mid_low = split_low(mid_ref[...])
    for block in range(2):
        rows = slice(block * packed, (block + 1) * packed)
        high, low = split_low(query_grad[rows])
        total += product(high, up_ref[block], 1, 1) + product(low, up_ref[block], 1, 1)
        every = product(mid_high, high, 0, 0) + product(mid_low, high, 0, 0)
        every += product(mid_high, low, 0, 0)
        raised += every[block * 2 * R : block * 2 * R + R]
        high, low = split_low(value_grad[rows])
        total += product(high, value_up_ref[block], 1, 1)
        total += product(low, value_up_ref[block], 1, 1)
        every = product(mid_high, high, 0, 0) + product(mid_low, high, 0, 0)
        every += product(mid_high, low, 0, 0)
        value_part += every[block * 2 * R + R : (block + 1) * 2 * R]
    factor_ref[...] = total.reshape(factor_ref.shape)
    raised = adapter_scale * raised
    value_part = adapter_scale * value_part
    raise_ref[...] = jnp.concatenate(
        [raised[:, at : at + 128] for at in range(0, width, 128)], axis=0
    ).reshape(raise_ref.shape)
    per = R // gx
    value_ref[...] = jnp.zeros_like(value_ref)
    for at in range(gx):
        value_ref[at, :per] = value_part[at * per : (at + 1) * per]

    spread(slots, slot_me, slot_device, lambda i: factor_ref.at[i], factor_recv.at[slot_me], sends.at[0], recvs.at[0])
    spread(gx, col, column_device, lambda i: value_ref.at[i], value_recv.at[col], sends.at[1], recvs.at[1])
    spread(gx, col, column_device, lambda i: raise_ref.at[i], raise_recv.at[col], sends.at[2], recvs.at[2])

    drain(factor_recv, recvs.at[0])
    factor_sum[...] = jnp.sum(factor_recv[...], axis=0)
    spread(slots, slot_me, slot_device, lambda i: factor_sum, factor_all.at[slot_me], sends.at[3], recvs.at[3])
    drain(value_recv, recvs.at[1])
    value_sum[...] = jnp.sum(value_recv[...], axis=0)
    spread(gz, place, place_device, lambda i: value_sum, value_plane.at[place], sends.at[4], recvs.at[4])
    drain(raise_recv, recvs.at[2])
    raise_sum[...] = jnp.sum(raise_recv[...], axis=0)
    spread(gx, col, column_device, lambda i: raise_sum, raise_all.at[col], sends.at[5], recvs.at[5])

    drain(factor_all, recvs.at[3])
    factor = factor_all[...].reshape(packed, 128)
    factor_high, factor_low = split_low(factor)

    def project(rows):
        block = li_ref[rows, :]
        dims = (((0,), (0,)), ((), ()))
        return lax.dot_general(
            block, factor_high, dims, preferred_element_type=jnp.float32
        ) + lax.dot_general(block, factor_low, dims, preferred_element_type=jnp.float32)

    first = project(slice(0, packed))
    second = project(slice(packed, 2 * packed))
    lane = lax.broadcasted_iota(jnp.int32, first.shape, 1)
    both = adapter_scale * jnp.where(lane < 64, first, second)
    both = both + pltpu.roll(both, 64, 1)
    rows = both.shape[0] // 2
    both = jnp.where(lane[:rows] < 64, both[:rows], both[rows:])
    down_part[...] = both.reshape(down_part.shape)
    spread(gx, col, column_device, lambda i: down_part.at[i], down_recv.at[col], sends.at[6], recvs.at[6])

    drain(value_plane, recvs.at[4])
    value_done[...] = jnp.sum(value_plane[...], axis=0)
    spread(gy, lev, level_device, lambda i: value_done, value_level.at[lev], sends.at[7], recvs.at[7])
    drain(value_level, recvs.at[7])
    spread(gx, col, column_device, lambda i: value_level, value_all.at[col], sends.at[8], recvs.at[8])

    drain(down_recv, recvs.at[6])
    down_sum[...] = jnp.sum(down_recv[...], axis=0)
    spread(gx, col, column_device, lambda i: down_sum, down_all.at[col], sends.at[9], recvs.at[9])

    drain(raise_all, recvs.at[5])
    raised = raise_all[...].reshape(-1, 128)
    for at in range(raised.shape[0] // R):
        out_ref[:, at * 128 : (at + 1) * 128] = raised[at * R : (at + 1) * R]
    drain(value_all, recvs.at[8])
    for at in range(gx):
        for level in range(gy):
            start = width + 2 * li_ref.shape[1] + level * 128
            out_ref[at * per : (at + 1) * per, start : start + 128] = value_all[at, level, :per]
    drain(down_all, recvs.at[9])
    turned = down_all[...].reshape(-1, 128).T
    for at, source in enumerate((0, 2, 1, 3)):
        start = width + at * rows
        out_ref[:, start : start + rows] = turned[source * R : (source + 1) * R]
    drain(factor_recv.at[: slots - 1], sends.at[0])
    drain(value_recv.at[: gx - 1], sends.at[1])
    drain(raise_recv.at[: gx - 1], sends.at[2])
    drain(factor_all.at[: slots - 1], sends.at[3])
    drain(value_plane.at[: gz - 1], sends.at[4])
    drain(raise_all.at[: gx - 1], sends.at[5])
    drain(down_recv.at[: gx - 1], sends.at[6])
    drain(value_level.at[: gy - 1], sends.at[7])
    drain(value_all.at[: gx - 1], sends.at[8])
    drain(down_all.at[: gx - 1], sends.at[9])


def whole_kernel(
    sizes,
    counts,
    lengths_ref,
    a_ref,
    w_ref,
    li_any,
    query_down_any,
    value_down_any,
    queries_any,
    keys_any,
    values_any,
    up_any,
    value_up_any,
    out_ref,
    *scratch,
):
    gx, gy, gz = sizes
    first, second = scratch[: counts[0]], scratch[counts[0] : counts[0] + counts[1]]
    grad_ref, mid_ref, queries_ref, keys_ref, values_ref = second[:5]
    up_ref, value_up_ref, attention_ref = second[5:8]
    in_sems = scratch[-1]
    seq, width = queries_any.shape
    kv = (lax.axis_index("gy") * gz + lax.axis_index("gz")) * (width // HD) // (HQ // KVH)
    kv_columns = pl.ds(pl.multiple_of(kv * HD, HD), HD)
    copies = [
        pltpu.make_async_copy(queries_any, queries_ref, in_sems.at[0]),
        pltpu.make_async_copy(keys_any.at[:, kv_columns], keys_ref, in_sems.at[1]),
        pltpu.make_async_copy(values_any.at[:, kv_columns], values_ref, in_sems.at[2]),
        pltpu.make_async_copy(up_any, up_ref.at[0, :R], in_sems.at[3]),
        pltpu.make_async_copy(up_any, up_ref.at[1, 2 * R : 3 * R], in_sems.at[4]),
        pltpu.make_async_copy(
            value_up_any.at[:, kv_columns], value_up_ref.at[0, R : 2 * R], in_sems.at[5]
        ),
        pltpu.make_async_copy(
            value_up_any.at[:, kv_columns], value_up_ref.at[1, 3 * R :], in_sems.at[6]
        ),
    ]

    def attend(step):
        if step == 0:
            for copy in copies:
                copy.start()
            up_ref[0, R:] = jnp.zeros((3 * R, width), jnp.bfloat16)
            up_ref[1, : 2 * R] = jnp.zeros((2 * R, width), jnp.bfloat16)
            up_ref[1, 3 * R :] = jnp.zeros((R, width), jnp.bfloat16)
            value_up_ref[0, :R] = jnp.zeros((R, HD), jnp.bfloat16)
            value_up_ref[0, 2 * R :] = jnp.zeros((2 * R, HD), jnp.bfloat16)
            value_up_ref[1, : 3 * R] = jnp.zeros((3 * R, HD), jnp.bfloat16)
            for copy in copies:
                copy.wait()
        steps = gy // 2
        heads = width // HD

        def one(head, carry):
            attention_kernel(lengths_ref, queries_ref, keys_ref, attention_ref, head)
            return carry

        lax.fori_loop(step * heads // steps, (step + 1) * heads // steps, one, 0)

    grad_kernel(
        sizes,
        a_ref,
        w_ref,
        li_any,
        query_down_any,
        value_down_any,
        grad_ref,
        mid_ref,
        *first,
        attend,
    )
    sum_kernel(
        sizes,
        lengths_ref,
        out_ref,
        first[0],
        grad_ref,
        mid_ref,
        keys_ref,
        values_ref,
        up_ref,
        value_up_ref,
        attention_ref,
        *second[8:],
    )


def part_kernel(whole_ref, *part_refs):
    start = 0
    for part_ref in part_refs:
        part_ref[...] = whole_ref[:, start : start + part_ref.shape[1]]
        start += part_ref.shape[1]


def body(
    sizes,
    out_grad,
    layer_input,
    out_weight,
    saved_queries,
    saved_keys,
    saved_values,
    query_down,
    query_up,
    value_down,
    value_up,
    lengths,
):
    gx, gy, gz = sizes
    seq, width = out_grad.shape
    heads, depth = out_weight.shape
    slots = gy * gz
    unit = seq // slots
    piece = seq // 2 // slots
    sides = gx // 2
    single, low = jnp.float32, jnp.bfloat16
    dma = pltpu.SemaphoreType.DMA
    first = [
        pltpu.VMEM((seq, width), low),
        pltpu.VMEM((2, 4 * R, width), low),
        pltpu.VMEM((gy, unit * gz, width), low),
        pltpu.VMEM((gz, gy, gx * unit, width), low),
        pltpu.VMEM((2, heads, depth), low),
        pltpu.VMEM((4, 2, heads // 4, depth), low),
        pltpu.VMEM((gz, gy, sides, 2, unit, heads), low),
        pltpu.VMEM((gz, gy, 2, unit, heads), single),
        pltpu.VMEM((sides - 1, gz, gy, 2, unit, heads), low),
        pltpu.VMEM((gz, gy, unit, heads), low),
        pltpu.VMEM((gz, gy, unit, heads), low),
        pltpu.VMEM((gz, gy, unit, heads), low),
        pltpu.VMEM((gz, gy, unit, heads), low),
        pltpu.VMEM((seq // 2, 128), single),
        pltpu.VMEM((slots, piece, 128), single),
        pltpu.VMEM((piece, 128), single),
        pltpu.VMEM((seq // 2, 128), single),
        dma((2, gy)),
        dma((2,)),
        dma((3,)),
        dma((2, 4)),
        dma((2, 4)),
        dma((2, gy - 1)),
        dma((2, gy - 1)),
        dma((1,)),
        dma((3,)),
        dma((3,)),
        dma((3,)),
        dma((2,)),
        dma((4,)),
        pltpu.SemaphoreType.REGULAR,
        dma((5,)),
    ]
    factor = (slots, piece, 128)
    raised = (gx, R * heads // 128 // gx, 128)
    value = (gx, max(ROWS, R // gx), 128)
    down = (gx, width // gx // 2, 128)
    shapes = [
        ((seq, heads), low),
        ((seq // 2, 128), single),
        ((seq, heads), low),
        ((seq, HD), low),
        ((seq, HD), low),
        ((2, 4 * R, heads), low),
        ((2, 4 * R, HD), low),
        ((heads // HD, seq, seq), single),
        ((seq, heads), single),
        ((seq, HD), single),
        (factor, single),
        (raised, single),
        (value, single),
        (factor, single),
        (factor[1:], single),
        (factor, single),
        (raised, single),
        (raised[1:], single),
        (raised, single),
        (value, single),
        (value[1:], single),
        ((gz,) + value[1:], single),
        (value[1:], single),
        ((gy,) + value[1:], single),
        ((gx, gy) + value[1:], single),
        (down, single),
        (down, single),
        (down[1:], single),
        (down, single),
    ]
    second = [pltpu.VMEM(shape, kind) for shape, kind in shapes] + [dma((10,)), dma((10,))]
    result = pl.pallas_call(
        functools.partial(whole_kernel, sizes, (len(first), len(second))),
        out_shape=jax.ShapeDtypeStruct((R, heads + 2 * width + gy * 128), single),
        in_specs=[pl.BlockSpec(memory_space=pltpu.SMEM)]
        + [pl.BlockSpec(memory_space=pl.ANY)] * 10,
        out_specs=pl.BlockSpec(memory_space=pltpu.VMEM),
        scratch_shapes=first + second + [dma((7,))],
        compiler_params=pltpu.CompilerParams(
            collective_id=0, has_side_effects=True, vmem_limit_bytes=60 << 20
        ),
        cost_estimate=pl.CostEstimate(
            flops=2 * seq * heads * depth * gx, bytes_accessed=16 << 20, transcendentals=0
        ),
    )(
        lengths,
        out_grad,
        out_weight,
        layer_input,
        query_down.T,
        value_down.T,
        saved_queries,
        saved_keys,
        saved_values,
        query_up,
        value_up,
    )
    parts = pl.pallas_call(
        part_kernel,
        out_shape=tuple(
            jax.ShapeDtypeStruct((R, count), single) for count in (heads, width, width, gy * 128)
        ),
    )(result)
    return (parts[1].T, parts[0], parts[2].T, parts[3])


def solution(mesh):
    sizes = tuple(mesh.shape[name] for name in ("gx", "gy", "gz"))
    return jax.shard_map(
        functools.partial(body, sizes),
        mesh=mesh,
        in_specs=(
            P("gx", ("gy", "gz")),
            P("gx", ("gy", "gz")),
            P(("gy", "gz"), "gx"),
            P("gx", ("gy", "gz")),
            P("gx", None),
            P("gx", None),
            P(("gy", "gz"), None),
            P(None, ("gy", "gz")),
            P(("gy", "gz"), None),
            P(),
            P("gx"),
        ),
        out_specs=(P(("gy", "gz"), None), P(None, ("gy", "gz")), P(("gy", "gz"), None), P()),
        check_vma=False,
    )
```

```python
import functools

import jax
import jax.numpy as jnp
from jax import lax
from jax.experimental import pallas as pl
from jax.experimental.pallas import tpu as pltpu
from jax.sharding import PartitionSpec as P

HQ = 128
KVH = 8
HD = 128
R = 32

adapter_scale = 2.0
mask_fill = -1e30
MESH = pl.DeviceIdType.MESH
ROWS = 8


def drain(ref, sem):
    pltpu.make_async_copy(ref, ref, sem).wait()


def send_to(src, dst, send_sem, recv_sem, device):
    return pltpu.make_async_remote_copy(
        src_ref=src,
        dst_ref=dst,
        send_sem=send_sem,
        recv_sem=recv_sem,
        device_id=device,
        device_id_type=MESH,
    )


def spread(count, me, device_of, src_of, dst, send_sem, recv_sem):
    pltpu.make_async_copy(src_of(me), dst, recv_sem).start()

    middle = count // 2

    def step(index, carry):
        offset = jnp.where(index < count - middle, middle + index, count - 1 - index)
        peer = lax.rem(me + offset, count)
        send_to(src_of(peer), dst, send_sem, recv_sem, device_of(peer)).start()
        return carry

    lax.fori_loop(0, count - 1, step, 0)


def greet(count, me, device_of):
    def step(offset, carry):
        peer = lax.rem(me + offset, count)
        pl.semaphore_signal(
            pltpu.get_barrier_semaphore(), inc=1, device_id=device_of(peer), device_id_type=MESH
        )
        return carry

    lax.fori_loop(1, count, step, 0)


def rows_of(index, count):
    return pl.ds(pl.multiple_of(index * count, count), count)


def grad_kernel(
    sizes,
    a_ref,
    w_ref,
    li_ref,
    query_ref,
    value_ref,
    out_ref,
    mid_ref,
    li_buf,
    dw_buf,
    t_buf,
    a_buf,
    w_buf,
    w_far,
    c_part,
    c_own,
    c_recv,
    x_send,
    x_recv,
    d_send,
    d_recv,
    mid_part,
    mid_recv,
    mid_sum,
    mid_all,
    t_sems,
    first_sems,
    w_sems,
    far_sems,
    twin_sems,
    ring_send,
    ring_recv,
    c_sems,
    c_arrived,
    x_sems,
    x_arrived,
    d_sems,
    m_sems,
    gate,
    in_sems,
    attend,
):
    gx, gy, gz = sizes
    col, lev, place = lax.axis_index("gx"), lax.axis_index("gy"), lax.axis_index("gz")
    far, core = place // 2, lax.rem(place, 2)
    sides = gx // 2
    near_x, side = col // sides, lax.rem(col, sides)
    slots = gy * gz
    slot_me = lev * gz + place
    seq, width = a_ref.shape
    heads = w_ref.shape[0]
    unit = seq // slots
    chunk = unit * gz
    last = gy // 2

    def slot_device(index):
        return (col, index // gz, lax.rem(index, gz))

    def plane_device(index):
        return (index // gz, lev, lax.rem(index, gz))

    copies = [
        pltpu.make_async_copy(li_ref, li_buf, in_sems.at[0]),
        pltpu.make_async_copy(query_ref, dw_buf.at[0, :R], in_sems.at[1]),
        pltpu.make_async_copy(value_ref, dw_buf.at[0, R : 2 * R], in_sems.at[2]),
        pltpu.make_async_copy(query_ref, dw_buf.at[1, 2 * R : 3 * R], in_sems.at[3]),
        pltpu.make_async_copy(value_ref, dw_buf.at[1, 3 * R :], in_sems.at[4]),
    ]
    for copy in copies:
        copy.start()
    none = jnp.zeros((2 * R, width), jnp.bfloat16)
    dw_buf[0, 2 * R :] = none
    dw_buf[1, : 2 * R] = none

    greet(slots, slot_me, slot_device)
    greet(gx * gz, col * gz + place, plane_device)

    pl.semaphore_wait(pltpu.get_barrier_semaphore(), slots - 1 + gx * gz - 1)

    def level_send(away):
        other = lax.rem(lev + away, gy)
        return send_to(
            a_ref.at[rows_of(other, chunk)],
            t_buf.at[lev],
            t_sems.at[0, away],
            t_sems.at[1, away],
            (col, other, place),
        )

    order = [last]
    for away in range(last - 1, 0, -1):
        order += [away, gy - away]
    for away in order:
        level_send(away).start()

    def column_send(to, block):
        def one(index, carry):
            at = lax.rem(place + index, gz)
            source = block.at[rows_of(at, unit)]
            target = a_buf.at[place, 0, rows_of(side * 2 + near_x, unit)]
            mine = jnp.logical_and(col == to, at == place)

            @pl.when(mine)
            def _():
                pltpu.make_async_copy(source, target, first_sems.at[1]).start()

            @pl.when(jnp.logical_not(mine))
            def _():
                send_to(
                    source, target, first_sems.at[0], first_sems.at[1], (to, lev, at)
                ).start()

            return carry

        lax.fori_loop(0, gz, one, 0)

    column_send(lev, a_ref.at[rows_of(lev, chunk)])

    sibling = (col, lev, far * 2 + 1 - core)
    opposite = (col, lev, (1 - far) * 2 + core)
    shares = 4
    band = heads // shares
    own_w = pltpu.make_async_copy(w_ref, w_buf.at[0], w_sems.at[0])
    own_w.start()
    twin_w = send_to(w_ref, w_buf.at[1], w_sems.at[1], w_sems.at[2], sibling)
    twin_w.start()

    def far_w(share):
        return send_to(
            w_ref.at[pl.ds(share * band, band)],
            w_far.at[share, 0],
            far_sems.at[0, share],
            far_sems.at[1, share],
            opposite,
        )

    def pass_w(share):
        return send_to(
            w_far.at[share, 0],
            w_far.at[share, 1],
            twin_sems.at[0, share],
            twin_sems.at[1, share],
            sibling,
        )

    far_w(0).start()

    for away in order:
        other = lax.rem(lev + gy - away, gy)
        level_send(away).wait_recv()
        column_send(other, t_buf.at[other])

    up = (col, lax.rem(lev + 1, gy), place)
    down = (col, lax.rem(lev + gy - 1, gy), place)

    def ring(way, hop, which):
        parts = slice(2 * which, 2 * which + 2)
        start = 2 * hop - 3 + way if hop > 1 else 0
        end = 2 * hop - 1 + (way if hop < last else 0)
        index = 2 * (hop - 1) + (which if hop < last else 0)
        return send_to(
            a_buf.at[parts, start],
            a_buf.at[parts, end],
            ring_send.at[way, index],
            ring_recv.at[way, index],
            (up, down)[way],
        )

    cut = gy - 2

    def products(start, steps, weights):
        total = jnp.zeros((steps * gx * unit, weights(0).shape[0]), jnp.float32)
        for part in range(gz):
            total += lax.dot_general(
                a_buf[part, start : start + steps].reshape(steps * gx * unit, width),
                weights(part),
                (((1,), (1,)), ((), ())),
                preferred_element_type=jnp.float32,
            )
        return total

    def keep(block, start, steps, columns, total):
        total = total.reshape(steps, sides, 2, unit, total.shape[1])
        c_part[block, start : start + steps, :, :, :, columns] = total.astype(jnp.bfloat16)
        for way in range(sides):

            @pl.when(side == way)
            def _():
                c_own[block, start : start + steps, :, :, columns] = total[:, way]

    def give(blocks, start, steps, columns, kind):
        for at, end, group in (
            (start, min(start + steps, cut), kind),
            (max(start, cut), start + steps, 1),
        ):
            if end > at:
                for away in range(1, sides):
                    other = lax.rem(side + away, sides)
                    send_to(
                        c_part.at[blocks, at:end, other, :, :, columns],
                        c_recv.at[away - 1, blocks, at:end, :, :, columns],
                        c_sems.at[0],
                        c_arrived.at[group],
                        (near_x * sides + other, lev, place),
                    ).start()

    def near(start, steps):
        def one_block(block, carry):
            total = products(
                start, steps, lambda part: w_buf[block, :, part * width : (part + 1) * width]
            )
            keep(block, start, steps, slice(0, heads), total)
            give(pl.ds(block, 1), start, steps, slice(0, heads), 0)
            return carry

        lax.fori_loop(0, 2, one_block, 0)

    def far_part(start, share):
        total = products(
            start,
            2,
            lambda part: w_far[share, :, :, part * width : (part + 1) * width].reshape(
                2 * band, width
            ),
        )
        columns = slice(share * band, (share + 1) * band)
        for index in range(2):
            keep(2 + index, start, 2, columns, total[:, index * band : (index + 1) * band])
        give(slice(2, 4), start, 2, columns, 2)

    drain(a_buf.at[: gz - 1, 0], first_sems.at[0])
    drain(a_buf.at[gz - 1, 0, : (gx - 1) * unit], first_sems.at[0])

    def gate_signal(offset, carry):
        peer = lax.rem(near_x * gz + place + offset, 2 * gz)
        pl.semaphore_signal(
            gate,
            inc=1,
            device_id=(peer // gz * sides + side, lev, lax.rem(peer, gz)),
            device_id_type=MESH,
        )
        return carry

    lax.fori_loop(1, 2 * gz, gate_signal, 0)
    attend(0)
    pl.semaphore_wait(gate, 2 * gz - 1)
    far_w(1).start()
    far_w(2).start()
    far_w(3).start()
    drain(a_buf.at[:, 0], first_sems.at[1])
    for which in range(2):
        for way in range(2):
            ring(way, 1, which).start()
    packed = seq // 2
    for copy in copies:
        copy.wait()
    lanes = (((1,), (1,)), ((), ()))
    mid_part[...] = lax.dot_general(
        li_buf[:packed, :], dw_buf[0], lanes, preferred_element_type=jnp.float32
    ) + lax.dot_general(li_buf[packed:, :], dw_buf[1], lanes, preferred_element_type=jnp.float32)

    piece = packed // slots
    spread(
        slots,
        slot_me,
        slot_device,
        lambda index: mid_part.at[rows_of(index, piece)],
        mid_recv.at[slot_me],
        m_sems.at[0],
        m_sems.at[1],
    )

    own_w.wait()
    twin_w.wait_recv()
    near(0, 1)
    attend(1)
    far_w(0).wait_recv()
    pass_w(0).start()
    for hop in range(1, last):
        for which in range(2):
            for way in range(2):
                ring(way, hop, which).wait_recv()
                if hop < last - 1 or way == which:
                    ring(way, hop + 1, which).start()
        near(2 * hop - 1, 2)
        if hop < last - 1:
            attend(hop + 1)
        if hop == 1:
            pass_w(0).wait_recv()
        for share in range(hop):
            far_part(2 * hop - 2, share)
        for share in [hop] if hop < last - 1 else range(hop, shares):
            far_w(share).wait_recv()
            pass_w(share).start()
            far_w(share).wait_send()
            pass_w(share).wait_recv()
            for start in range(0, 2 * hop, 2):
                far_part(start, share)
        if hop == max(1, last - 2):
            drain(mid_recv, m_sems.at[1])
            mid_sum[...] = jnp.sum(mid_recv[...], axis=0)
            spread(
                slots,
                slot_me,
                slot_device,
                lambda index: mid_sum,
                mid_all.at[rows_of(slot_me, piece)],
                m_sems.at[2],
                m_sems.at[3],
            )
    ring(0, last, 0).wait_recv()
    ring(1, last, 1).wait_recv()
    near(gy - 1, 1)
    for share in range(shares):
        far_part(gy - 2, share)

    def hand_over(low, high, start, end, group):
        drain(c_recv.at[:, low:high, start:end], c_arrived.at[group])

        def one(block, carry):
            total = c_own[block, start:end]
            for away in range(sides - 1):
                total += c_recv[away, block, start:end].astype(jnp.float32)
            for half in range(2):

                @pl.when(near_x == half)
                def _():
                    x_send[block, start:end] = total[:, 1 - half].astype(jnp.bfloat16)
                    c_own[block, start:end, 0] = total[:, half]

            return carry

        lax.fori_loop(low, high, one, 0)
        send_to(
            x_send.at[low:high, start:end],
            x_recv.at[low:high, start:end],
            x_sems.at[group],
            x_arrived.at[group],
            ((1 - near_x) * sides + side, lev, place),
        ).start()

    def hand_out(low, high, start, end, group):
        drain(x_recv.at[low:high, start:end], x_arrived.at[group])

        def one(block, carry):
            total = c_own[block, start:end, 0] + x_recv[block, start:end].astype(jnp.float32)
            d_send[block, start:end] = total.astype(jnp.bfloat16)
            return carry

        lax.fori_loop(low, high, one, 0)
        for block in range(low, high):
            if block == 0:
                d_recv[place, start:end] = d_send[0, start:end]
                continue
            at = (far if block < 2 else 1 - far) * 2 + (1 - core if block % 2 else core)
            send_to(
                d_send.at[block, start:end],
                d_recv.at[place, start:end],
                d_sems.at[0],
                d_sems.at[1],
                (col, lev, at),
            ).start()

    hand_over(0, 2, 0, cut, 0)
    hand_over(2, 4, 0, cut, 2)
    hand_out(0, 2, 0, cut, 0)
    hand_over(0, 4, cut, gy, 1)
    hand_out(2, 4, 0, cut, 2)
    hand_out(0, 4, cut, gy, 1)

    for away in order:
        level_send(away).wait_send()
    twin_w.wait_send()
    far_w(0).wait_send()
    for share in range(shares):
        pass_w(share).wait_send()
    for hop in range(1, last + 1):
        for which in range(2):
            for way in range(2):
                if hop < last or way == which:
                    ring(way, hop, which).wait_send()
    drain(mid_recv.at[: slots - 1], m_sems.at[0])
    drain(mid_recv.at[: slots - 1], m_sems.at[2])
    drain(mid_all, m_sems.at[3])
    mid_ref[...] = mid_all[...]
    drain(c_part.at[:, : gy * (sides - 1) // sides], c_sems.at[0])
    drain(x_send.at[:2, :cut], x_sems.at[0])
    drain(x_send.at[:, cut:], x_sems.at[1])
    drain(x_send.at[2:, :cut], x_sems.at[2])
    drain(d_send.at[1:], d_sems.at[0])
    drain(d_send.at[1:], d_sems.at[1])

    for start in range(gy):
        hop = (start + 1) // 2
        level = lax.rem(lev + (gy - hop if start % 2 else hop), gy)

        def one_place(at, carry):
            out_ref[rows_of(level * gz + at, unit), :] = d_recv[at, start]
            return carry

        lax.fori_loop(0, gz, one_place, 0)


def split_low(array):
    high = array.astype(jnp.bfloat16)
    return high, (array - high.astype(jnp.float32)).astype(jnp.bfloat16)


def product(left, right, left_dim, right_dim):
    return lax.dot_general(
        left, right, (((left_dim,), (right_dim,)), ((), ())), preferred_element_type=jnp.float32
    )


def attention_kernel(
    lengths_ref,
    queries_ref,
    keys_ref,
    attention_ref,
    head,
):
    seq = queries_ref.shape[0]
    packed = seq // 2
    length = lengths_ref[0]
    columns = pl.ds(pl.multiple_of(head * HD, HD), HD)
    for block in range(2):
        rows = slice(block * packed, (block + 1) * packed)
        span = (block + 1) * packed
        shape = (packed, span)
        row = lax.broadcasted_iota(jnp.int32, shape, 0) + block * packed
        key = lax.broadcasted_iota(jnp.int32, shape, 1)
        scores = product(queries_ref[rows, columns], keys_ref[:span], 1, 1) * HD ** (-0.5)
        scores = jnp.where((key <= row) & (key < length), scores, mask_fill)
        raised = jnp.exp(scores - jnp.max(scores, axis=1, keepdims=True))
        attention_ref[head, rows, :span] = raised / jnp.sum(raised, axis=1, keepdims=True)


def sum_kernel(
    sizes,
    lengths_ref,
    out_ref,
    li_ref,
    grad_ref,
    mid_ref,
    keys_ref,
    values_ref,
    up_ref,
    value_up_ref,
    attention_ref,
    query_grad,
    value_grad,
    factor_ref,
    raise_ref,
    value_ref,
    factor_recv,
    factor_sum,
    factor_all,
    raise_recv,
    raise_sum,
    raise_all,
    value_recv,
    value_sum,
    value_plane,
    value_done,
    value_level,
    value_all,
    down_part,
    down_recv,
    down_sum,
    down_all,
    sends,
    recvs,
):
    gx, gy, gz = sizes
    col, lev, place = lax.axis_index("gx"), lax.axis_index("gy"), lax.axis_index("gz")
    slots = gy * gz
    slot_me = lev * gz + place
    seq, width = query_grad.shape
    packed = seq // 2
    length = lengths_ref[0]

    def slot_device(index):
        return (col, index // gz, lax.rem(index, gz))

    def column_device(index):
        return (index, lev, place)

    def level_device(index):
        return (col, index, place)

    def place_device(index):
        return (col, lev, index)

    value_grad[...] = jnp.zeros_like(value_grad)

    def one_head(head, carry):
        columns = pl.ds(pl.multiple_of(head * HD, HD), HD)
        for block in range(2):
            rows = slice(block * packed, (block + 1) * packed)
            span = (block + 1) * packed
            attention = attention_ref[head, rows, :span]
            grads = grad_ref[rows, columns]
            line = lax.broadcasted_iota(jnp.int32, grads.shape, 0) + block * packed
            grads = jnp.where(line < length, grads.astype(jnp.float32), 0.0).astype(jnp.bfloat16)
            value_grad[:span] += product(attention.astype(jnp.bfloat16), grads, 0, 0)
            prob_grad = product(grads, values_ref[:span], 1, 1)
            centre = jnp.sum(attention * prob_grad, axis=1, keepdims=True)
            score_grad = (attention * (prob_grad - centre)).astype(jnp.bfloat16)
            query_grad[rows, columns] = product(score_grad, keys_ref[:span], 1, 0) * HD ** (-0.5)
        return carry

    lax.fori_loop(0, width // HD, one_head, 0)

    total = jnp.zeros((packed, 128), jnp.float32)
    raised = jnp.zeros((R, width), jnp.float32)
    value_part = jnp.zeros((R, HD), jnp.float32)
    mid_high, mid_low = split_low(mid_ref[...])
    for block in range(2):
        rows = slice(block * packed, (block + 1) * packed)
        high, low = split_low(query_grad[rows])
        total += product(high, up_ref[block], 1, 1) + product(low, up_ref[block], 1, 1)
        every = product(mid_high, high, 0, 0) + product(mid_low, high, 0, 0)
        every += product(mid_high, low, 0, 0)
        raised += every[block * 2 * R : block * 2 * R + R]
        high, low = split_low(value_grad[rows])
        total += product(high, value_up_ref[block], 1, 1)
        total += product(low, value_up_ref[block], 1, 1)
        every = product(mid_high, high, 0, 0) + product(mid_low, high, 0, 0)
        every += product(mid_high, low, 0, 0)
        value_part += every[block * 2 * R + R : (block + 1) * 2 * R]
    factor_ref[...] = total.reshape(factor_ref.shape)
    raised = adapter_scale * raised
    value_part = adapter_scale * value_part
    raise_ref[...] = jnp.concatenate(
        [raised[:, at : at + 128] for at in range(0, width, 128)], axis=0
    ).reshape(raise_ref.shape)
    per = R // gx
    value_ref[...] = jnp.zeros_like(value_ref)
    for at in range(gx):
        value_ref[at, :per] = value_part[at * per : (at + 1) * per]

    spread(slots, slot_me, slot_device, lambda i: factor_ref.at[i], factor_recv.at[slot_me], sends.at[0], recvs.at[0])
    spread(gx, col, column_device, lambda i: value_ref.at[i], value_recv.at[col], sends.at[1], recvs.at[1])
    spread(gx, col, column_device, lambda i: raise_ref.at[i], raise_recv.at[col], sends.at[2], recvs.at[2])

    drain(factor_recv, recvs.at[0])
    factor_sum[...] = jnp.sum(factor_recv[...], axis=0)
    spread(slots, slot_me, slot_device, lambda i: factor_sum, factor_all.at[slot_me], sends.at[3], recvs.at[3])
    drain(value_recv, recvs.at[1])
    value_sum[...] = jnp.sum(value_recv[...], axis=0)
    spread(gz, place, place_device, lambda i: value_sum, value_plane.at[place], sends.at[4], recvs.at[4])
    drain(raise_recv, recvs.at[2])
    raise_sum[...] = jnp.sum(raise_recv[...], axis=0)
    spread(gx, col, column_device, lambda i: raise_sum, raise_all.at[col], sends.at[5], recvs.at[5])

    drain(factor_all, recvs.at[3])
    factor = factor_all[...].reshape(packed, 128)
    factor_high, factor_low = split_low(factor)

    def project(rows):
        block = li_ref[rows, :]
        dims = (((0,), (0,)), ((), ()))
        return lax.dot_general(
            block, factor_high, dims, preferred_element_type=jnp.float32
        ) + lax.dot_general(block, factor_low, dims, preferred_element_type=jnp.float32)

    first = project(slice(0, packed))
    second = project(slice(packed, 2 * packed))
    lane = lax.broadcasted_iota(jnp.int32, first.shape, 1)
    both = adapter_scale * jnp.where(lane < 64, first, second)
    both = both + pltpu.roll(both, 64, 1)
    rows = both.shape[0] // 2
    both = jnp.where(lane[:rows] < 64, both[:rows], both[rows:])
    down_part[...] = both.reshape(down_part.shape)
    spread(gx, col, column_device, lambda i: down_part.at[i], down_recv.at[col], sends.at[6], recvs.at[6])

    drain(value_plane, recvs.at[4])
    value_done[...] = jnp.sum(value_plane[...], axis=0)
    spread(gy, lev, level_device, lambda i: value_done, value_level.at[lev], sends.at[7], recvs.at[7])
    drain(value_level, recvs.at[7])
    spread(gx, col, column_device, lambda i: value_level, value_all.at[col], sends.at[8], recvs.at[8])

    drain(down_recv, recvs.at[6])
    down_sum[...] = jnp.sum(down_recv[...], axis=0)
    spread(gx, col, column_device, lambda i: down_sum, down_all.at[col], sends.at[9], recvs.at[9])

    drain(raise_all, recvs.at[5])
    raised = raise_all[...].reshape(-1, 128)
    for at in range(raised.shape[0] // R):
        out_ref[:, at * 128 : (at + 1) * 128] = raised[at * R : (at + 1) * R]
    drain(value_all, recvs.at[8])
    for at in range(gx):
        for level in range(gy):
            start = width + 2 * li_ref.shape[1] + level * 128
            out_ref[at * per : (at + 1) * per, start : start + 128] = value_all[at, level, :per]
    drain(down_all, recvs.at[9])
    turned = down_all[...].reshape(-1, 128).T
    for at, source in enumerate((0, 2, 1, 3)):
        start = width + at * rows
        out_ref[:, start : start + rows] = turned[source * R : (source + 1) * R]
    drain(factor_recv.at[: slots - 1], sends.at[0])
    drain(value_recv.at[: gx - 1], sends.at[1])
    drain(raise_recv.at[: gx - 1], sends.at[2])
    drain(factor_all.at[: slots - 1], sends.at[3])
    drain(value_plane.at[: gz - 1], sends.at[4])
    drain(raise_all.at[: gx - 1], sends.at[5])
    drain(down_recv.at[: gx - 1], sends.at[6])
    drain(value_level.at[: gy - 1], sends.at[7])
    drain(value_all.at[: gx - 1], sends.at[8])
    drain(down_all.at[: gx - 1], sends.at[9])


def whole_kernel(
    sizes,
    counts,
    lengths_ref,
    a_ref,
    w_ref,
    li_any,
    query_down_any,
    value_down_any,
    queries_any,
    keys_any,
    values_any,
    up_any,
    value_up_any,
    out_ref,
    *scratch,
):
    gx, gy, gz = sizes
    first, second = scratch[: counts[0]], scratch[counts[0] : counts[0] + counts[1]]
    grad_ref, mid_ref, queries_ref, keys_ref, values_ref = second[:5]
    up_ref, value_up_ref, attention_ref = second[5:8]
    in_sems = scratch[-1]
    seq, width = queries_any.shape
    kv = (lax.axis_index("gy") * gz + lax.axis_index("gz")) * (width // HD) // (HQ // KVH)
    kv_columns = pl.ds(pl.multiple_of(kv * HD, HD), HD)
    copies = [
        pltpu.make_async_copy(queries_any, queries_ref, in_sems.at[0]),
        pltpu.make_async_copy(keys_any.at[:, kv_columns], keys_ref, in_sems.at[1]),
        pltpu.make_async_copy(values_any.at[:, kv_columns], values_ref, in_sems.at[2]),
        pltpu.make_async_copy(up_any, up_ref.at[0, :R], in_sems.at[3]),
        pltpu.make_async_copy(up_any, up_ref.at[1, 2 * R : 3 * R], in_sems.at[4]),
        pltpu.make_async_copy(
            value_up_any.at[:, kv_columns], value_up_ref.at[0, R : 2 * R], in_sems.at[5]
        ),
        pltpu.make_async_copy(
            value_up_any.at[:, kv_columns], value_up_ref.at[1, 3 * R :], in_sems.at[6]
        ),
    ]

    def attend(step):
        if step == 0:
            up_ref[0, R:] = jnp.zeros((3 * R, width), jnp.bfloat16)
            up_ref[1, : 2 * R] = jnp.zeros((2 * R, width), jnp.bfloat16)
            up_ref[1, 3 * R :] = jnp.zeros((R, width), jnp.bfloat16)
            value_up_ref[0, :R] = jnp.zeros((R, HD), jnp.bfloat16)
            value_up_ref[0, 2 * R :] = jnp.zeros((2 * R, HD), jnp.bfloat16)
            value_up_ref[1, : 3 * R] = jnp.zeros((3 * R, HD), jnp.bfloat16)
            for copy in copies:
                copy.wait()
        steps = gy // 2
        heads = width // HD

        def one(head, carry):
            attention_kernel(lengths_ref, queries_ref, keys_ref, attention_ref, head)
            return carry

        lax.fori_loop(step * heads // steps, (step + 1) * heads // steps, one, 0)

    for copy in copies:
        copy.start()
    grad_kernel(
        sizes,
        a_ref,
        w_ref,
        li_any,
        query_down_any,
        value_down_any,
        grad_ref,
        mid_ref,
        *first,
        attend,
    )
    sum_kernel(
        sizes,
        lengths_ref,
        out_ref,
        first[0],
        grad_ref,
        mid_ref,
        keys_ref,
        values_ref,
        up_ref,
        value_up_ref,
        attention_ref,
        *second[8:],
    )


def part_kernel(whole_ref, *part_refs):
    start = 0
    for part_ref in part_refs:
        part_ref[...] = whole_ref[:, start : start + part_ref.shape[1]]
        start += part_ref.shape[1]


def body(
    sizes,
    out_grad,
    layer_input,
    out_weight,
    saved_queries,
    saved_keys,
    saved_values,
    query_down,
    query_up,
    value_down,
    value_up,
    lengths,
):
    gx, gy, gz = sizes
    seq, width = out_grad.shape
    heads, depth = out_weight.shape
    slots = gy * gz
    unit = seq // slots
    piece = seq // 2 // slots
    sides = gx // 2
    single, low = jnp.float32, jnp.bfloat16
    dma = pltpu.SemaphoreType.DMA
    first = [
        pltpu.VMEM((seq, width), low),
        pltpu.VMEM((2, 4 * R, width), low),
        pltpu.VMEM((gy, unit * gz, width), low),
        pltpu.VMEM((gz, gy, gx * unit, width), low),
        pltpu.VMEM((2, heads, depth), low),
        pltpu.VMEM((4, 2, heads // 4, depth), low),
        pltpu.VMEM((gz, gy, sides, 2, unit, heads), low),
        pltpu.VMEM((gz, gy, 2, unit, heads), single),
        pltpu.VMEM((sides - 1, gz, gy, 2, unit, heads), low),
        pltpu.VMEM((gz, gy, unit, heads), low),
        pltpu.VMEM((gz, gy, unit, heads), low),
        pltpu.VMEM((gz, gy, unit, heads), low),
        pltpu.VMEM((gz, gy, unit, heads), low),
        pltpu.VMEM((seq // 2, 128), single),
        pltpu.VMEM((slots, piece, 128), single),
        pltpu.VMEM((piece, 128), single),
        pltpu.VMEM((seq // 2, 128), single),
        dma((2, gy)),
        dma((2,)),
        dma((3,)),
        dma((2, 4)),
        dma((2, 4)),
        dma((2, gy - 1)),
        dma((2, gy - 1)),
        dma((1,)),
        dma((3,)),
        dma((3,)),
        dma((3,)),
        dma((2,)),
        dma((4,)),
        pltpu.SemaphoreType.REGULAR,
        dma((5,)),
    ]
    factor = (slots, piece, 128)
    raised = (gx, R * heads // 128 // gx, 128)
    value = (gx, max(ROWS, R // gx), 128)
    down = (gx, width // gx // 2, 128)
    shapes = [
        ((seq, heads), low),
        ((seq // 2, 128), single),
        ((seq, heads), low),
        ((seq, HD), low),
        ((seq, HD), low),
        ((2, 4 * R, heads), low),
        ((2, 4 * R, HD), low),
        ((heads // HD, seq, seq), single),
        ((seq, heads), single),
        ((seq, HD), single),
        (factor, single),
        (raised, single),
        (value, single),
        (factor, single),
        (factor[1:], single),
        (factor, single),
        (raised, single),
        (raised[1:], single),
        (raised, single),
        (value, single),
        (value[1:], single),
        ((gz,) + value[1:], single),
        (value[1:], single),
        ((gy,) + value[1:], single),
        ((gx, gy) + value[1:], single),
        (down, single),
        (down, single),
        (down[1:], single),
        (down, single),
    ]
    second = [pltpu.VMEM(shape, kind) for shape, kind in shapes] + [dma((10,)), dma((10,))]
    result = pl.pallas_call(
        functools.partial(whole_kernel, sizes, (len(first), len(second))),
        out_shape=jax.ShapeDtypeStruct((R, heads + 2 * width + gy * 128), single),
        in_specs=[pl.BlockSpec(memory_space=pltpu.SMEM)]
        + [pl.BlockSpec(memory_space=pl.ANY)] * 10,
        out_specs=pl.BlockSpec(memory_space=pltpu.VMEM),
        scratch_shapes=first + second + [dma((7,))],
        compiler_params=pltpu.CompilerParams(
            collective_id=0, has_side_effects=True, vmem_limit_bytes=60 << 20
        ),
        cost_estimate=pl.CostEstimate(
            flops=2 * seq * heads * depth * gx, bytes_accessed=16 << 20, transcendentals=0
        ),
    )(
        lengths,
        out_grad,
        out_weight,
        layer_input,
        query_down.T,
        value_down.T,
        saved_queries,
        saved_keys,
        saved_values,
        query_up,
        value_up,
    )
    parts = pl.pallas_call(
        part_kernel,
        out_shape=tuple(
            jax.ShapeDtypeStruct((R, count), single) for count in (heads, width, width, gy * 128)
        ),
    )(result)
    return (parts[1].T, parts[0], parts[2].T, parts[3])


def solution(mesh):
    sizes = tuple(mesh.shape[name] for name in ("gx", "gy", "gz"))
    return jax.shard_map(
        functools.partial(body, sizes),
        mesh=mesh,
        in_specs=(
            P("gx", ("gy", "gz")),
            P("gx", ("gy", "gz")),
            P(("gy", "gz"), "gx"),
            P("gx", ("gy", "gz")),
            P("gx", None),
            P("gx", None),
            P(("gy", "gz"), None),
            P(None, ("gy", "gz")),
            P(("gy", "gz"), None),
            P(),
            P("gx"),
        ),
        out_specs=(P(("gy", "gz"), None), P(None, ("gy", "gz")), P(("gy", "gz"), None), P()),
        check_vma=False,
    )
```

```python
import functools

import jax
import jax.numpy as jnp
from jax import lax
from jax.experimental import pallas as pl
from jax.experimental.pallas import tpu as pltpu
from jax.sharding import PartitionSpec as P

HQ = 128
KVH = 8
HD = 128
R = 32

adapter_scale = 2.0
mask_fill = -1e30
MESH = pl.DeviceIdType.MESH
ROWS = 8


def drain(ref, sem):
    pltpu.make_async_copy(ref, ref, sem).wait()


def send_to(src, dst, send_sem, recv_sem, device):
    return pltpu.make_async_remote_copy(
        src_ref=src,
        dst_ref=dst,
        send_sem=send_sem,
        recv_sem=recv_sem,
        device_id=device,
        device_id_type=MESH,
    )


def spread(count, me, device_of, src_of, dst, send_sem, recv_sem):
    pltpu.make_async_copy(src_of(me), dst, recv_sem).start()

    middle = count // 2

    def step(index, carry):
        offset = jnp.where(index < count - middle, middle + index, count - 1 - index)
        peer = lax.rem(me + offset, count)
        send_to(src_of(peer), dst, send_sem, recv_sem, device_of(peer)).start()
        return carry

    lax.fori_loop(0, count - 1, step, 0)


def greet(count, me, device_of):
    def step(offset, carry):
        peer = lax.rem(me + offset, count)
        pl.semaphore_signal(
            pltpu.get_barrier_semaphore(), inc=1, device_id=device_of(peer), device_id_type=MESH
        )
        return carry

    lax.fori_loop(1, count, step, 0)


def rows_of(index, count):
    return pl.ds(pl.multiple_of(index * count, count), count)


def grad_kernel(
    sizes,
    a_ref,
    w_ref,
    li_ref,
    query_ref,
    value_ref,
    out_ref,
    mid_ref,
    li_buf,
    dw_buf,
    t_buf,
    a_buf,
    w_buf,
    w_far,
    c_part,
    c_own,
    c_recv,
    x_send,
    x_recv,
    d_send,
    d_recv,
    mid_part,
    mid_recv,
    mid_sum,
    mid_all,
    t_sems,
    first_sems,
    w_sems,
    far_sems,
    twin_sems,
    ring_send,
    ring_recv,
    c_sems,
    c_arrived,
    x_sems,
    x_arrived,
    d_sems,
    m_sems,
    gate,
    in_sems,
    attend,
):
    gx, gy, gz = sizes
    col, lev, place = lax.axis_index("gx"), lax.axis_index("gy"), lax.axis_index("gz")
    far, core = place // 2, lax.rem(place, 2)
    sides = gx // 2
    near_x, side = col // sides, lax.rem(col, sides)
    slots = gy * gz
    slot_me = lev * gz + place
    seq, width = a_ref.shape
    heads = w_ref.shape[0]
    unit = seq // slots
    chunk = unit * gz
    last = gy // 2

    def slot_device(index):
        return (col, index // gz, lax.rem(index, gz))

    def plane_device(index):
        return (index // gz, lev, lax.rem(index, gz))

    copies = [
        pltpu.make_async_copy(li_ref, li_buf, in_sems.at[0]),
        pltpu.make_async_copy(query_ref, dw_buf.at[0, :R], in_sems.at[1]),
        pltpu.make_async_copy(value_ref, dw_buf.at[0, R : 2 * R], in_sems.at[2]),
        pltpu.make_async_copy(query_ref, dw_buf.at[1, 2 * R : 3 * R], in_sems.at[3]),
        pltpu.make_async_copy(value_ref, dw_buf.at[1, 3 * R :], in_sems.at[4]),
    ]
    for copy in copies:
        copy.start()
    none = jnp.zeros((2 * R, width), jnp.bfloat16)
    dw_buf[0, 2 * R :] = none
    dw_buf[1, : 2 * R] = none

    greet(slots, slot_me, slot_device)
    greet(gx * gz, col * gz + place, plane_device)

    pl.semaphore_wait(pltpu.get_barrier_semaphore(), slots - 1 + gx * gz - 1)

    def level_send(away):
        other = lax.rem(lev + away, gy)
        return send_to(
            a_ref.at[rows_of(other, chunk)],
            t_buf.at[lev],
            t_sems.at[0, away],
            t_sems.at[1, away],
            (col, other, place),
        )

    order = [last]
    for away in range(last - 1, 0, -1):
        order += [away, gy - away]
    for away in order:
        level_send(away).start()

    def column_send(to, block):
        def one(index, carry):
            at = lax.rem(place + index, gz)
            source = block.at[rows_of(at, unit)]
            target = a_buf.at[place, 0, rows_of(side * 2 + near_x, unit)]
            mine = jnp.logical_and(col == to, at == place)

            @pl.when(mine)
            def _():
                pltpu.make_async_copy(source, target, first_sems.at[1]).start()

            @pl.when(jnp.logical_not(mine))
            def _():
                send_to(
                    source, target, first_sems.at[0], first_sems.at[1], (to, lev, at)
                ).start()

            return carry

        lax.fori_loop(0, gz, one, 0)

    column_send(lev, a_ref.at[rows_of(lev, chunk)])

    sibling = (col, lev, far * 2 + 1 - core)
    opposite = (col, lev, (1 - far) * 2 + core)
    shares = 4
    band = heads // shares
    own_w = pltpu.make_async_copy(w_ref, w_buf.at[0], w_sems.at[0])
    own_w.start()
    twin_w = send_to(w_ref, w_buf.at[1], w_sems.at[1], w_sems.at[2], sibling)
    twin_w.start()

    def far_w(share):
        return send_to(
            w_ref.at[pl.ds(share * band, band)],
            w_far.at[share, 0],
            far_sems.at[0, share],
            far_sems.at[1, share],
            opposite,
        )

    def pass_w(share):
        return send_to(
            w_far.at[share, 0],
            w_far.at[share, 1],
            twin_sems.at[0, share],
            twin_sems.at[1, share],
            sibling,
        )

    far_w(0).start()

    for away in order:
        other = lax.rem(lev + gy - away, gy)
        level_send(away).wait_recv()
        column_send(other, t_buf.at[other])

    up = (col, lax.rem(lev + 1, gy), place)
    down = (col, lax.rem(lev + gy - 1, gy), place)

    def ring(way, hop, which):
        parts = slice(2 * which, 2 * which + 2)
        start = 2 * hop - 3 + way if hop > 1 else 0
        end = 2 * hop - 1 + (way if hop < last else 0)
        index = 2 * (hop - 1) + (which if hop < last else 0)
        return send_to(
            a_buf.at[parts, start],
            a_buf.at[parts, end],
            ring_send.at[way, index],
            ring_recv.at[way, index],
            (up, down)[way],
        )

    cut = gy - 2

    def products(start, steps, weights):
        total = jnp.zeros((steps * gx * unit, weights(0).shape[0]), jnp.float32)
        for part in range(gz):
            total += lax.dot_general(
                a_buf[part, start : start + steps].reshape(steps * gx * unit, width),
                weights(part),
                (((1,), (1,)), ((), ())),
                preferred_element_type=jnp.float32,
            )
        return total

    def keep(block, start, steps, columns, total):
        total = total.reshape(steps, sides, 2, unit, total.shape[1])
        c_part[block, start : start + steps, :, :, :, columns] = total.astype(jnp.bfloat16)
        for way in range(sides):

            @pl.when(side == way)
            def _():
                c_own[block, start : start + steps, :, :, columns] = total[:, way]

    def give(blocks, start, steps, columns, kind):
        for at, end, group in (
            (start, min(start + steps, cut), kind),
            (max(start, cut), start + steps, 1),
        ):
            if end > at:
                for away in range(1, sides):
                    other = lax.rem(side + away, sides)
                    send_to(
                        c_part.at[blocks, at:end, other, :, :, columns],
                        c_recv.at[away - 1, blocks, at:end, :, :, columns],
                        c_sems.at[0],
                        c_arrived.at[group],
                        (near_x * sides + other, lev, place),
                    ).start()

    def near(start, steps):
        def one_block(block, carry):
            total = products(
                start, steps, lambda part: w_buf[block, :, part * width : (part + 1) * width]
            )
            keep(block, start, steps, slice(0, heads), total)
            give(pl.ds(block, 1), start, steps, slice(0, heads), 0)
            return carry

        lax.fori_loop(0, 2, one_block, 0)

    def far_part(start, share):
        total = products(
            start,
            2,
            lambda part: w_far[share, :, :, part * width : (part + 1) * width].reshape(
                2 * band, width
            ),
        )
        columns = slice(share * band, (share + 1) * band)
        for index in range(2):
            keep(2 + index, start, 2, columns, total[:, index * band : (index + 1) * band])
        give(slice(2, 4), start, 2, columns, 2)

    drain(a_buf.at[: gz - 1, 0], first_sems.at[0])
    drain(a_buf.at[gz - 1, 0, : (gx - 1) * unit], first_sems.at[0])

    def gate_signal(offset, carry):
        peer = lax.rem(near_x * gz + place + offset, 2 * gz)
        pl.semaphore_signal(
            gate,
            inc=1,
            device_id=(peer // gz * sides + side, lev, lax.rem(peer, gz)),
            device_id_type=MESH,
        )
        return carry

    lax.fori_loop(1, 2 * gz, gate_signal, 0)
    attend(0)
    pl.semaphore_wait(gate, 2 * gz - 1)
    far_w(1).start()
    far_w(2).start()
    far_w(3).start()
    drain(a_buf.at[:, 0], first_sems.at[1])
    for which in range(2):
        for way in range(2):
            ring(way, 1, which).start()
    packed = seq // 2
    for copy in copies:
        copy.wait()
    lanes = (((1,), (1,)), ((), ()))
    mid_part[...] = lax.dot_general(
        li_buf[:packed, :], dw_buf[0], lanes, preferred_element_type=jnp.float32
    ) + lax.dot_general(li_buf[packed:, :], dw_buf[1], lanes, preferred_element_type=jnp.float32)

    piece = packed // slots
    spread(
        slots,
        slot_me,
        slot_device,
        lambda index: mid_part.at[rows_of(index, piece)],
        mid_recv.at[slot_me],
        m_sems.at[0],
        m_sems.at[1],
    )

    own_w.wait()
    twin_w.wait_recv()
    near(0, 1)
    attend(1)
    far_w(0).wait_recv()
    pass_w(0).start()
    for hop in range(1, last):
        for which in range(2):
            for way in range(2):
                ring(way, hop, which).wait_recv()
                if hop < last - 1 or way == which:
                    ring(way, hop + 1, which).start()
        near(2 * hop - 1, 2)
        if hop < last - 1:
            attend(hop + 1)
        if hop == 1:
            pass_w(0).wait_recv()
        for share in range(hop):
            far_part(2 * hop - 2, share)
        for share in [hop] if hop < last - 1 else range(hop, shares):
            far_w(share).wait_recv()
            pass_w(share).start()
            far_w(share).wait_send()
            pass_w(share).wait_recv()
            for start in range(0, 2 * hop, 2):
                far_part(start, share)
        if hop == max(1, last - 2):
            drain(mid_recv, m_sems.at[1])
            mid_sum[...] = jnp.sum(mid_recv[...], axis=0)
            spread(
                slots,
                slot_me,
                slot_device,
                lambda index: mid_sum,
                mid_all.at[rows_of(slot_me, piece)],
                m_sems.at[2],
                m_sems.at[3],
            )
    ring(0, last, 0).wait_recv()
    ring(1, last, 1).wait_recv()
    near(gy - 1, 1)
    for share in range(shares):
        far_part(gy - 2, share)

    def hand_over(low, high, start, end, group):
        drain(c_recv.at[:, low:high, start:end], c_arrived.at[group])

        def one(block, carry):
            total = c_own[block, start:end]
            for away in range(sides - 1):
                total += c_recv[away, block, start:end].astype(jnp.float32)
            for half in range(2):

                @pl.when(near_x == half)
                def _():
                    x_send[block, start:end] = total[:, 1 - half].astype(jnp.bfloat16)
                    c_own[block, start:end, 0] = total[:, half]

            return carry

        lax.fori_loop(low, high, one, 0)
        send_to(
            x_send.at[low:high, start:end],
            x_recv.at[low:high, start:end],
            x_sems.at[group],
            x_arrived.at[group],
            ((1 - near_x) * sides + side, lev, place),
        ).start()

    def hand_out(low, high, start, end, group):
        drain(x_recv.at[low:high, start:end], x_arrived.at[group])

        def one(block, carry):
            total = c_own[block, start:end, 0] + x_recv[block, start:end].astype(jnp.float32)
            d_send[block, start:end] = total.astype(jnp.bfloat16)
            return carry

        lax.fori_loop(low, high, one, 0)
        for block in range(low, high):
            if block == 0:
                d_recv[place, start:end] = d_send[0, start:end]
                continue
            at = (far if block < 2 else 1 - far) * 2 + (1 - core if block % 2 else core)
            send_to(
                d_send.at[block, start:end],
                d_recv.at[place, start:end],
                d_sems.at[0],
                d_sems.at[1],
                (col, lev, at),
            ).start()

    hand_over(0, 2, 0, cut, 0)
    hand_over(2, 4, 0, cut, 2)
    hand_out(0, 2, 0, cut, 0)
    hand_over(0, 4, cut, gy, 1)
    hand_out(2, 4, 0, cut, 2)
    hand_out(0, 4, cut, gy, 1)

    for away in order:
        level_send(away).wait_send()
    twin_w.wait_send()
    far_w(0).wait_send()
    for share in range(shares):
        pass_w(share).wait_send()
    for hop in range(1, last + 1):
        for which in range(2):
            for way in range(2):
                if hop < last or way == which:
                    ring(way, hop, which).wait_send()
    drain(mid_recv.at[: slots - 1], m_sems.at[0])
    drain(mid_recv.at[: slots - 1], m_sems.at[2])
    drain(mid_all, m_sems.at[3])
    mid_ref[...] = mid_all[...]
    drain(c_part.at[:, : gy * (sides - 1) // sides], c_sems.at[0])
    drain(x_send.at[:2, :cut], x_sems.at[0])
    drain(x_send.at[:, cut:], x_sems.at[1])
    drain(x_send.at[2:, :cut], x_sems.at[2])
    drain(d_send.at[1:], d_sems.at[0])
    drain(d_send.at[1:], d_sems.at[1])

    for start in range(gy):
        hop = (start + 1) // 2
        level = lax.rem(lev + (gy - hop if start % 2 else hop), gy)

        def one_place(at, carry):
            out_ref[rows_of(level * gz + at, unit), :] = d_recv[at, start]
            return carry

        lax.fori_loop(0, gz, one_place, 0)


def split_low(array):
    high = array.astype(jnp.bfloat16)
    return high, (array - high.astype(jnp.float32)).astype(jnp.bfloat16)


def product(left, right, left_dim, right_dim):
    return lax.dot_general(
        left, right, (((left_dim,), (right_dim,)), ((), ())), preferred_element_type=jnp.float32
    )


def attention_kernel(
    lengths_ref,
    queries_ref,
    keys_ref,
    attention_ref,
    head,
):
    seq = queries_ref.shape[0]
    packed = seq // 2
    length = lengths_ref[0]
    columns = pl.ds(pl.multiple_of(head * HD, HD), HD)
    for block in range(2):
        rows = slice(block * packed, (block + 1) * packed)
        span = (block + 1) * packed
        shape = (packed, span)
        row = lax.broadcasted_iota(jnp.int32, shape, 0) + block * packed
        key = lax.broadcasted_iota(jnp.int32, shape, 1)
        scores = product(queries_ref[rows, columns], keys_ref[:span], 1, 1) * HD ** (-0.5)
        scores = jnp.where((key <= row) & (key < length), scores, mask_fill)
        raised = jnp.exp(scores - jnp.max(scores, axis=1, keepdims=True))
        attention_ref[head, rows, :span] = raised / jnp.sum(raised, axis=1, keepdims=True)


def sum_kernel(
    sizes,
    lengths_ref,
    out_ref,
    li_ref,
    grad_ref,
    mid_ref,
    keys_ref,
    values_ref,
    up_ref,
    value_up_ref,
    attention_ref,
    query_grad,
    value_grad,
    factor_ref,
    raise_ref,
    value_ref,
    factor_recv,
    factor_sum,
    factor_all,
    raise_recv,
    raise_sum,
    raise_all,
    value_recv,
    value_sum,
    value_plane,
    value_done,
    value_level,
    value_all,
    down_part,
    down_recv,
    down_sum,
    down_all,
    sends,
    recvs,
):
    gx, gy, gz = sizes
    col, lev, place = lax.axis_index("gx"), lax.axis_index("gy"), lax.axis_index("gz")
    slots = gy * gz
    slot_me = lev * gz + place
    seq, width = query_grad.shape
    packed = seq // 2
    length = lengths_ref[0]

    def slot_device(index):
        return (col, index // gz, lax.rem(index, gz))

    def column_device(index):
        return (index, lev, place)

    def level_device(index):
        return (col, index, place)

    def place_device(index):
        return (col, lev, index)

    value_grad[...] = jnp.zeros_like(value_grad)

    def one_head(head, carry):
        columns = pl.ds(pl.multiple_of(head * HD, HD), HD)
        for block in range(2):
            rows = slice(block * packed, (block + 1) * packed)
            span = (block + 1) * packed
            attention = attention_ref[head, rows, :span]
            grads = grad_ref[rows, columns]
            line = lax.broadcasted_iota(jnp.int32, grads.shape, 0) + block * packed
            grads = jnp.where(line < length, grads.astype(jnp.float32), 0.0).astype(jnp.bfloat16)
            value_grad[:span] += product(attention.astype(jnp.bfloat16), grads, 0, 0)
            prob_grad = product(grads, values_ref[:span], 1, 1)
            centre = jnp.sum(attention * prob_grad, axis=1, keepdims=True)
            score_grad = (attention * (prob_grad - centre)).astype(jnp.bfloat16)
            query_grad[rows, columns] = product(score_grad, keys_ref[:span], 1, 0) * HD ** (-0.5)
        return carry

    lax.fori_loop(0, width // HD, one_head, 0)

    total = jnp.zeros((packed, 128), jnp.float32)
    raised = jnp.zeros((R, width), jnp.float32)
    value_part = jnp.zeros((R, HD), jnp.float32)
    mid_high, mid_low = split_low(mid_ref[...])
    for block in range(2):
        rows = slice(block * packed, (block + 1) * packed)
        high, low = split_low(query_grad[rows])
        total += product(high, up_ref[block], 1, 1) + product(low, up_ref[block], 1, 1)
        every = product(mid_high, high, 0, 0) + product(mid_low, high, 0, 0)
        every += product(mid_high, low, 0, 0)
        raised += every[block * 2 * R : block * 2 * R + R]
        high, low = split_low(value_grad[rows])
        total += product(high, value_up_ref[block], 1, 1)
        total += product(low, value_up_ref[block], 1, 1)
        every = product(mid_high, high, 0, 0) + product(mid_low, high, 0, 0)
        every += product(mid_high, low, 0, 0)
        value_part += every[block * 2 * R + R : (block + 1) * 2 * R]
    factor_ref[...] = total.reshape(factor_ref.shape)
    raised = adapter_scale * raised
    value_part = adapter_scale * value_part
    raise_ref[...] = jnp.concatenate(
        [raised[:, at : at + 128] for at in range(0, width, 128)], axis=0
    ).reshape(raise_ref.shape)
    per = R // gx
    value_ref[...] = jnp.zeros_like(value_ref)
    for at in range(gx):
        value_ref[at, :per] = value_part[at * per : (at + 1) * per]

    spread(slots, slot_me, slot_device, lambda i: factor_ref.at[i], factor_recv.at[slot_me], sends.at[0], recvs.at[0])
    spread(gx, col, column_device, lambda i: value_ref.at[i], value_recv.at[col], sends.at[1], recvs.at[1])
    spread(gx, col, column_device, lambda i: raise_ref.at[i], raise_recv.at[col], sends.at[2], recvs.at[2])

    drain(factor_recv, recvs.at[0])
    factor_sum[...] = jnp.sum(factor_recv[...], axis=0)
    spread(slots, slot_me, slot_device, lambda i: factor_sum, factor_all.at[slot_me], sends.at[3], recvs.at[3])
    drain(value_recv, recvs.at[1])
    value_sum[...] = jnp.sum(value_recv[...], axis=0)
    spread(gz, place, place_device, lambda i: value_sum, value_plane.at[place], sends.at[4], recvs.at[4])
    drain(raise_recv, recvs.at[2])
    raise_sum[...] = jnp.sum(raise_recv[...], axis=0)
    spread(gx, col, column_device, lambda i: raise_sum, raise_all.at[col], sends.at[5], recvs.at[5])

    drain(value_plane, recvs.at[4])
    value_done[...] = jnp.sum(value_plane[...], axis=0)
    spread(gy, lev, level_device, lambda i: value_done, value_level.at[lev], sends.at[7], recvs.at[7])

    drain(factor_all, recvs.at[3])
    factor = factor_all[...].reshape(packed, 128)
    factor_high, factor_low = split_low(factor)

    def project(rows):
        block = li_ref[rows, :]
        dims = (((0,), (0,)), ((), ()))
        return lax.dot_general(
            block, factor_high, dims, preferred_element_type=jnp.float32
        ) + lax.dot_general(block, factor_low, dims, preferred_element_type=jnp.float32)

    first = project(slice(0, packed))
    second = project(slice(packed, 2 * packed))
    lane = lax.broadcasted_iota(jnp.int32, first.shape, 1)
    both = adapter_scale * jnp.where(lane < 64, first, second)
    both = both + pltpu.roll(both, 64, 1)
    rows = both.shape[0] // 2
    both = jnp.where(lane[:rows] < 64, both[:rows], both[rows:])
    down_part[...] = both.reshape(down_part.shape)
    spread(gx, col, column_device, lambda i: down_part.at[i], down_recv.at[col], sends.at[6], recvs.at[6])

    drain(value_level, recvs.at[7])
    spread(gx, col, column_device, lambda i: value_level, value_all.at[col], sends.at[8], recvs.at[8])

    drain(down_recv, recvs.at[6])
    down_sum[...] = jnp.sum(down_recv[...], axis=0)
    spread(gx, col, column_device, lambda i: down_sum, down_all.at[col], sends.at[9], recvs.at[9])

    drain(raise_all, recvs.at[5])
    raised = raise_all[...].reshape(-1, 128)
    for at in range(raised.shape[0] // R):
        out_ref[:, at * 128 : (at + 1) * 128] = raised[at * R : (at + 1) * R]
    drain(value_all, recvs.at[8])
    for at in range(gx):
        for level in range(gy):
            start = width + 2 * li_ref.shape[1] + level * 128
            out_ref[at * per : (at + 1) * per, start : start + 128] = value_all[at, level, :per]
    drain(down_all, recvs.at[9])
    turned = down_all[...].reshape(-1, 128).T
    for at, source in enumerate((0, 2, 1, 3)):
        start = width + at * rows
        out_ref[:, start : start + rows] = turned[source * R : (source + 1) * R]
    drain(factor_recv.at[: slots - 1], sends.at[0])
    drain(value_recv.at[: gx - 1], sends.at[1])
    drain(raise_recv.at[: gx - 1], sends.at[2])
    drain(factor_all.at[: slots - 1], sends.at[3])
    drain(value_plane.at[: gz - 1], sends.at[4])
    drain(raise_all.at[: gx - 1], sends.at[5])
    drain(down_recv.at[: gx - 1], sends.at[6])
    drain(value_level.at[: gy - 1], sends.at[7])
    drain(value_all.at[: gx - 1], sends.at[8])
    drain(down_all.at[: gx - 1], sends.at[9])


def whole_kernel(
    sizes,
    counts,
    lengths_ref,
    a_ref,
    w_ref,
    li_any,
    query_down_any,
    value_down_any,
    queries_any,
    keys_any,
    values_any,
    up_any,
    value_up_any,
    out_ref,
    *scratch,
):
    gx, gy, gz = sizes
    first, second = scratch[: counts[0]], scratch[counts[0] : counts[0] + counts[1]]
    grad_ref, mid_ref, queries_ref, keys_ref, values_ref = second[:5]
    up_ref, value_up_ref, attention_ref = second[5:8]
    in_sems = scratch[-1]
    seq, width = queries_any.shape
    kv = (lax.axis_index("gy") * gz + lax.axis_index("gz")) * (width // HD) // (HQ // KVH)
    kv_columns = pl.ds(pl.multiple_of(kv * HD, HD), HD)
    copies = [
        pltpu.make_async_copy(queries_any, queries_ref, in_sems.at[0]),
        pltpu.make_async_copy(keys_any.at[:, kv_columns], keys_ref, in_sems.at[1]),
        pltpu.make_async_copy(values_any.at[:, kv_columns], values_ref, in_sems.at[2]),
        pltpu.make_async_copy(up_any, up_ref.at[0, :R], in_sems.at[3]),
        pltpu.make_async_copy(up_any, up_ref.at[1, 2 * R : 3 * R], in_sems.at[4]),
        pltpu.make_async_copy(
            value_up_any.at[:, kv_columns], value_up_ref.at[0, R : 2 * R], in_sems.at[5]
        ),
        pltpu.make_async_copy(
            value_up_any.at[:, kv_columns], value_up_ref.at[1, 3 * R :], in_sems.at[6]
        ),
    ]

    def attend(step):
        if step == 0:
            up_ref[0, R:] = jnp.zeros((3 * R, width), jnp.bfloat16)
            up_ref[1, : 2 * R] = jnp.zeros((2 * R, width), jnp.bfloat16)
            up_ref[1, 3 * R :] = jnp.zeros((R, width), jnp.bfloat16)
            value_up_ref[0, :R] = jnp.zeros((R, HD), jnp.bfloat16)
            value_up_ref[0, 2 * R :] = jnp.zeros((2 * R, HD), jnp.bfloat16)
            value_up_ref[1, : 3 * R] = jnp.zeros((3 * R, HD), jnp.bfloat16)
            for copy in copies:
                copy.wait()
        steps = gy // 2
        heads = width // HD

        def one(head, carry):
            attention_kernel(lengths_ref, queries_ref, keys_ref, attention_ref, head)
            return carry

        lax.fori_loop(step * heads // steps, (step + 1) * heads // steps, one, 0)

    for copy in copies:
        copy.start()
    grad_kernel(
        sizes,
        a_ref,
        w_ref,
        li_any,
        query_down_any,
        value_down_any,
        grad_ref,
        mid_ref,
        *first,
        attend,
    )
    sum_kernel(
        sizes,
        lengths_ref,
        out_ref,
        first[0],
        grad_ref,
        mid_ref,
        keys_ref,
        values_ref,
        up_ref,
        value_up_ref,
        attention_ref,
        *second[8:],
    )


def part_kernel(whole_ref, *part_refs):
    start = 0
    for part_ref in part_refs:
        part_ref[...] = whole_ref[:, start : start + part_ref.shape[1]]
        start += part_ref.shape[1]


def body(
    sizes,
    out_grad,
    layer_input,
    out_weight,
    saved_queries,
    saved_keys,
    saved_values,
    query_down,
    query_up,
    value_down,
    value_up,
    lengths,
):
    gx, gy, gz = sizes
    seq, width = out_grad.shape
    heads, depth = out_weight.shape
    slots = gy * gz
    unit = seq // slots
    piece = seq // 2 // slots
    sides = gx // 2
    single, low = jnp.float32, jnp.bfloat16
    dma = pltpu.SemaphoreType.DMA
    first = [
        pltpu.VMEM((seq, width), low),
        pltpu.VMEM((2, 4 * R, width), low),
        pltpu.VMEM((gy, unit * gz, width), low),
        pltpu.VMEM((gz, gy, gx * unit, width), low),
        pltpu.VMEM((2, heads, depth), low),
        pltpu.VMEM((4, 2, heads // 4, depth), low),
        pltpu.VMEM((gz, gy, sides, 2, unit, heads), low),
        pltpu.VMEM((gz, gy, 2, unit, heads), single),
        pltpu.VMEM((sides - 1, gz, gy, 2, unit, heads), low),
        pltpu.VMEM((gz, gy, unit, heads), low),
        pltpu.VMEM((gz, gy, unit, heads), low),
        pltpu.VMEM((gz, gy, unit, heads), low),
        pltpu.VMEM((gz, gy, unit, heads), low),
        pltpu.VMEM((seq // 2, 128), single),
        pltpu.VMEM((slots, piece, 128), single),
        pltpu.VMEM((piece, 128), single),
        pltpu.VMEM((seq // 2, 128), single),
        dma((2, gy)),
        dma((2,)),
        dma((3,)),
        dma((2, 4)),
        dma((2, 4)),
        dma((2, gy - 1)),
        dma((2, gy - 1)),
        dma((1,)),
        dma((3,)),
        dma((3,)),
        dma((3,)),
        dma((2,)),
        dma((4,)),
        pltpu.SemaphoreType.REGULAR,
        dma((5,)),
    ]
    factor = (slots, piece, 128)
    raised = (gx, R * heads // 128 // gx, 128)
    value = (gx, max(ROWS, R // gx), 128)
    down = (gx, width // gx // 2, 128)
    shapes = [
        ((seq, heads), low),
        ((seq // 2, 128), single),
        ((seq, heads), low),
        ((seq, HD), low),
        ((seq, HD), low),
        ((2, 4 * R, heads), low),
        ((2, 4 * R, HD), low),
        ((heads // HD, seq, seq), single),
        ((seq, heads), single),
        ((seq, HD), single),
        (factor, single),
        (raised, single),
        (value, single),
        (factor, single),
        (factor[1:], single),
        (factor, single),
        (raised, single),
        (raised[1:], single),
        (raised, single),
        (value, single),
        (value[1:], single),
        ((gz,) + value[1:], single),
        (value[1:], single),
        ((gy,) + value[1:], single),
        ((gx, gy) + value[1:], single),
        (down, single),
        (down, single),
        (down[1:], single),
        (down, single),
    ]
    second = [pltpu.VMEM(shape, kind) for shape, kind in shapes] + [dma((10,)), dma((10,))]
    result = pl.pallas_call(
        functools.partial(whole_kernel, sizes, (len(first), len(second))),
        out_shape=jax.ShapeDtypeStruct((R, heads + 2 * width + gy * 128), single),
        in_specs=[pl.BlockSpec(memory_space=pltpu.SMEM)]
        + [pl.BlockSpec(memory_space=pl.ANY)] * 10,
        out_specs=pl.BlockSpec(memory_space=pltpu.VMEM),
        scratch_shapes=first + second + [dma((7,))],
        compiler_params=pltpu.CompilerParams(
            collective_id=0, has_side_effects=True, vmem_limit_bytes=60 << 20
        ),
        cost_estimate=pl.CostEstimate(
            flops=2 * seq * heads * depth * gx, bytes_accessed=16 << 20, transcendentals=0
        ),
    )(
        lengths,
        out_grad,
        out_weight,
        layer_input,
        query_down.T,
        value_down.T,
        saved_queries,
        saved_keys,
        saved_values,
        query_up,
        value_up,
    )
    parts = pl.pallas_call(
        part_kernel,
        out_shape=tuple(
            jax.ShapeDtypeStruct((R, count), single) for count in (heads, width, width, gy * 128)
        ),
    )(result)
    return (parts[1].T, parts[0], parts[2].T, parts[3])


def solution(mesh):
    sizes = tuple(mesh.shape[name] for name in ("gx", "gy", "gz"))
    return jax.shard_map(
        functools.partial(body, sizes),
        mesh=mesh,
        in_specs=(
            P("gx", ("gy", "gz")),
            P("gx", ("gy", "gz")),
            P(("gy", "gz"), "gx"),
            P("gx", ("gy", "gz")),
            P("gx", None),
            P("gx", None),
            P(("gy", "gz"), None),
            P(None, ("gy", "gz")),
            P(("gy", "gz"), None),
            P(),
            P("gx"),
        ),
        out_specs=(P(("gy", "gz"), None), P(None, ("gy", "gz")), P(("gy", "gz"), None), P()),
        check_vma=False,
    )
```
